512 devices in a mesh: ctx: 32 (over z, core), fsdp: 16 (over x, y).
Axes of the slice: x: 4, y: 4, z: 16, core: 2. Of those that a mesh axis runs over, the one named last changes fastest.
Arguments:
- tokens: bfloat16 [8192, 4096], P('ctx', 'fsdp'), may hold values from -6 to 6
- w_xz: bfloat16 [4096, 32, 256], P('ctx', 'fsdp'), may hold values from -0.09375 to 0.09375
- w_bc: bfloat16 [4096, 256], P('ctx'), may hold values from -0.09375 to 0.09375
- gain: float32 [32, 128], P('fsdp'), may hold values from 0.5 to 1.5
- skip: float32 [32], P('fsdp'), may hold values from 0.5 to 2
- decays: float32 [32, 8192], P('fsdp', 'ctx'), may hold values from 0.4 to 1
- boundaries: int32 [8192], P('ctx'), may hold values 0 or 1
Outputs:
- mixed: bfloat16 [8192, 32, 128], P('ctx', 'fsdp')
The draws below stay inside these ranges and needn't reach their ends.
All inputs are finite; a program needn't handle non-finite values. No bound on the sum of `boundaries` on one device may be relied on, other than what follows from the above.
Results may differ from the reference program's by a relative error of at most 0.013.
Values may be sent and summed in bfloat16 or wider, within the bound.
No kernel may reach another device: no remote copies, remote signals or barrier semaphores. Data moves between devices by JAX's collectives and lax.ppermute only.
A program may use at most 64 MiB of HBM per device.

```python
import math
import jax
import jax.numpy as jnp
from jax import lax

D = 4096
HEAD_DIM = 128
STATE = 128
GROUP = 256
TOK_DEV = 256
HEADS = 32
SAMPLE_SLOTS = 8192


def draw_decays(key, part):
    key = jax.random.fold_in(key, 7)
    keys = jax.random.split(key, 6)
    fast_share = 0.5
    rough_guess = jnp.exp(jax.random.uniform(keys[2], (HEADS, SAMPLE_SLOTS), minval=math.log(0.5), maxval=math.log(2.0)))
    is_fast = jax.random.uniform(keys[0], (HEADS, 1)) < fast_share
    fast_rate = jnp.exp(jax.random.uniform(keys[1], (HEADS, 1), minval=math.log(1.0 / 50.0), maxval=math.log(1.0 / 30.0)))
    slow_rate = jnp.exp(jax.random.uniform(keys[3], (HEADS, 1), minval=math.log(0.2), maxval=math.log(1.5))) / SAMPLE_SLOTS
    stride_rate = jnp.where(is_fast, fast_rate, slow_rate)
    location_numbers = jax.random.randint(keys[4], (3,), 0, SAMPLE_SLOTS)
    spike_duration = jnp.any(jnp.arange(SAMPLE_SLOTS)[None, :] == location_numbers[:, None], axis=0)
    missing_samples = jax.random.uniform(keys[5], (HEADS, SAMPLE_SLOTS), minval=0.5, maxval=0.8)
    shrink_exponent = -stride_rate * rough_guess + jnp.where(spike_duration[None, :], jnp.log(missing_samples), 0.0)
    return jnp.exp(shrink_exponent).astype(jnp.float32)


def set_ends(drawn, stream_key, low, top_value):
    longest = drawn.shape.index(max(drawn.shape))
    spots = []
    for shift in (0, 1):
        where = [jax.random.randint(jax.random.fold_in(stream_key, axis), (), 0, length) for axis, length in enumerate(drawn.shape)]
        where[longest] = (where[longest] + shift) % drawn.shape[longest]
        spots.append(tuple(where))
    return drawn.at[spots[0]].set(low).at[spots[1]].set(top_value)


def steps_of(stream_key, extent, shards, low, top_value):
    loudness = 1.0
    for dim, parts in shards:
        draws = jax.random.uniform(jax.random.fold_in(jax.random.fold_in(stream_key, 6), dim), (parts,), jnp.float32, low / len(shards), top_value / len(shards))
        loudness = loudness * jnp.repeat(jnp.exp(draws), extent[dim] // parts).reshape((-1,) + (1,) * (len(extent) - 1 - dim))
    return loudness


def normal_values(stream_key, extent, width, most, cuts=(), held_as=jnp.bfloat16):
    drawn = jax.random.normal(stream_key, extent, jnp.float32) * width
    if len(cuts) > 0:
        drawn = steps_of(stream_key, extent, cuts, -0.22, 0.18) * drawn
    return jnp.clip(drawn, min=-most, max=most).astype(held_as)


def setup_inputs(seed: int = 0) -> dict:
    seeds = jax.random.split(jax.random.key(seed), 8)
    tokens = normal_values(seeds[0], (SAMPLE_SLOTS, D), 1.0, 6.0, ((0, 32), (1, 16)))
    w_xz = normal_values(seeds[1], (D, HEADS, 2 * HEAD_DIM), D ** -0.5, 0.09375, ((0, 32), (1, 16)))
    w_bc = normal_values(seeds[2], (D, 2 * STATE), D ** -0.5, 0.09375, ((0, 32),))
    gain = jnp.clip(1.0 + 0.1 * jax.random.normal(seeds[3], (HEADS, HEAD_DIM), jnp.float32), 0.5, 1.5)
    skip = jnp.clip(jnp.exp(math.log(2.0) - 1.3862944 * jax.random.uniform(seeds[4], (HEADS,), jnp.float32) ** steps_of(seeds[4], (HEADS,), ((0, 16),), -0.2, 0.2)), 0.5, 2.0)
    decays = draw_decays(jax.random.fold_in(seeds[7], 71), 0)
    boundaries = set_ends((jax.random.randint(seeds[6], (SAMPLE_SLOTS,), 0, 2 * TOK_DEV) < 1).astype(jnp.int32), jax.random.fold_in(seeds[6], 1), 0, 1)
    return dict(tokens=tokens, w_xz=w_xz, w_bc=w_bc, gain=gain, skip=skip, decays=decays, boundaries=boundaries)


def block_step(state_now, inputs):
    values, b_proj, c_proj, shrink_exponent, starts = inputs
    position = jnp.arange(GROUP)
    lower_ones = (position[:, None] >= position[None, :]).astype(jnp.float32)
    cumulative = jnp.dot(shrink_exponent, lower_ones.T, precision=lax.Precision.HIGHEST)
    segment_ids = jnp.cumsum(starts).astype(jnp.int32)
    allowed = (segment_ids[:, None] == segment_ids[None, :]) & (position[:, None] >= position[None, :])
    decay_mat = jnp.where(allowed[None], jnp.exp(cumulative[:, :, None] - cumulative[:, None, :]), 0.0)
    scores = jnp.dot(c_proj, b_proj.T, preferred_element_type=jnp.float32)
    weights = (decay_mat * scores[None]).astype(jnp.bfloat16)
    value_f = values.astype(jnp.float32)
    diagonal = jnp.einsum('hij,jhp->ihp', weights.astype(jnp.float32), value_f)
    last_total = cumulative[:, -1]
    last_segment = segment_ids[-1]
    to_end = jnp.where((segment_ids == last_segment)[None, :], jnp.exp(last_total[:, None] - cumulative), 0.0)
    scaled = (to_end.T[:, :, None] * value_f).astype(jnp.bfloat16)
    local_state = jnp.einsum('jhp,jn->hpn', scaled.astype(jnp.float32), b_proj.astype(jnp.float32))
    carry_in = jnp.where((segment_ids == 0)[None, :], jnp.exp(cumulative), 0.0)
    offdiag = jnp.einsum('in,hpn->ihp', c_proj.astype(jnp.float32), state_now, precision=lax.Precision.HIGHEST)
    offdiag = offdiag * carry_in.T[:, :, None]
    carry_gate = jnp.where(last_segment == 0, jnp.exp(last_total), 0.0)
    state_next = carry_gate[:, None, None] * state_now + local_state
    return (state_next, diagonal + offdiag)

def reference(tokens, w_xz, w_bc, gain, skip, decays, boundaries):
    proj = jnp.dot(tokens, w_xz.reshape(D, HEADS * 2 * HEAD_DIM), preferred_element_type=jnp.float32)
    proj = proj.reshape(SAMPLE_SLOTS, HEADS, 2, HEAD_DIM)
    values = jax.nn.silu(proj[:, :, 0]).astype(jnp.bfloat16)
    gate = proj[:, :, 1].astype(jnp.bfloat16)
    maps = jax.nn.silu(jnp.dot(tokens, w_bc, preferred_element_type=jnp.float32)).astype(jnp.bfloat16)
    blocks = SAMPLE_SLOTS // GROUP
    shrink_exponent = jnp.log(decays).reshape(HEADS, blocks, GROUP).transpose(1, 0, 2)
    inputs = (values.reshape(blocks, GROUP, HEADS, HEAD_DIM), maps[:, :STATE].reshape(blocks, GROUP, STATE), maps[:, STATE:].reshape(blocks, GROUP, STATE), shrink_exponent, boundaries.reshape(blocks, GROUP))
    start_state = jnp.zeros((HEADS, HEAD_DIM, STATE), jnp.float32)
    final_state, output = lax.scan(block_step, start_state, inputs)
    output = output.reshape(SAMPLE_SLOTS, HEADS, HEAD_DIM) + skip[None, :, None] * values.astype(jnp.float32)
    gated = output * jax.nn.silu(gate.astype(jnp.float32))
    mean_square = lax.optimization_barrier(jnp.mean(gated * gated, axis=(1, 2)))
    normed = gated * lax.rsqrt(mean_square + 1e-05)[:, None, None] * gain[None]
    return normed.astype(jnp.bfloat16)
```

```python
import jax
import jax.numpy as jnp
from jax import lax
from jax.sharding import PartitionSpec as P

F32 = jnp.float32
BF16 = jnp.bfloat16


def swap_cores(x, count):
    return lax.ppermute(x, "ctx", [(i, i ^ 1) for i in range(count)])


def to_all(x, axis):
    size = lax.axis_size(axis)
    return lax.all_to_all(jnp.broadcast_to(x[None], (size,) + x.shape), axis, 0, 0)


def per_device(tokens, w_xz, w_bc, gain, skip, decays, boundaries):
    rows = tokens.shape[0]
    heads = w_xz.shape[1]
    width = w_xz.shape[2] // 2
    n_state = w_bc.shape[1] // 2
    n_ctx, n_fsdp = lax.axis_size("ctx"), lax.axis_size("fsdp")
    n_chip = n_ctx // 2
    ctx, fsdp = lax.axis_index("ctx"), lax.axis_index("fsdp")
    core, chip = ctx % 2, ctx // 2
    same_core = [[2 * z + c for z in range(n_chip)] for c in range(2)]

    w_all = lax.all_gather(w_xz.reshape(w_xz.shape[0], -1), "ctx", axis=0, tiled=True)
    tok = to_all(tokens, "fsdp")
    share = w_bc.shape[1] // n_fsdp
    part = lax.dynamic_slice_in_dim(w_bc.T, fsdp * share, share, axis=0)
    part = lax.all_gather(part, "ctx", axis=0, axis_index_groups=same_core)
    other = swap_cores(part, n_ctx)
    even, odd = jnp.where(core == 0, part, other), jnp.where(core == 0, other, part)
    part = jnp.stack([even, odd], axis=1)
    part = part.transpose(2, 0, 1, 3).reshape(share, n_fsdp, -1)
    maps_t = jnp.einsum("sfk,fik->si", part, tok, preferred_element_type=F32)
    maps_t = jax.nn.silu(maps_t).astype(BF16)
    maps_t = to_all(maps_t, "fsdp").reshape(2, n_state, rows)
    b_t, c_t = maps_t[0], maps_t[1]

    position = jnp.arange(rows)
    causal = position[:, None] >= position[None, :]
    cum = jnp.einsum(
        "hj,ij->hi", jnp.log(decays), causal.astype(F32), precision=lax.Precision.HIGHEST
    )
    seg = jnp.cumsum(boundaries)
    allowed = (seg[:, None] == seg[None, :]) & causal
    decay = jnp.where(allowed[None], jnp.exp(cum[:, :, None] - cum[:, None, :]), 0.0)
    scores = jnp.einsum("ni,nj->ij", c_t, b_t, preferred_element_type=F32)
    weights = (decay * scores[None]).astype(BF16)
    total, last = cum[:, -1], seg[-1]
    to_end = jnp.where((seg == last)[None], jnp.exp(total[:, None] - cum), 0.0)
    carry_in = jnp.where((seg == 0)[None], jnp.exp(cum), 0.0)
    gate_end = jnp.where(last == 0, jnp.exp(total), 0.0)

    proj = jnp.einsum(
        "fik,fkn->in", tok, w_all.reshape(n_fsdp, -1, w_all.shape[1]), preferred_element_type=F32
    )
    proj = proj.reshape(rows, heads, 2, width)
    values = jax.nn.silu(proj[:, :, 0]).astype(BF16)
    gate = proj[:, :, 1].astype(BF16)
    value_f = values.astype(F32)
    scaled = (to_end.T[:, :, None] * value_f).astype(BF16)
    local = jnp.einsum("jhp,nj->hpn", scaled, b_t, preferred_element_type=F32)

    tail = jnp.broadcast_to(gate_end[:, None, None], (heads, 8, n_state))
    mine = jnp.concatenate([local, tail], axis=1)
    keep = jnp.where(core == 0, mine[0], mine[1])
    got = swap_cores(jnp.where(core == 0, mine[1], mine[0]), n_ctx)
    first, second = jnp.where(core == 0, keep, got), jnp.where(core == 0, got, keep)
    s0, g0, s1, g1 = first[:width], first[width, 0], second[:width], second[width, 0]
    s_chip, g_chip = g1 * s0 + s1, g0 * g1
    g_hi = g_chip.astype(BF16)
    g_mid = (g_chip - g_hi.astype(F32)).astype(BF16)
    g_lo = (g_chip - g_hi.astype(F32) - g_mid.astype(F32)).astype(BF16)
    g_row = jnp.stack([g_hi, g_mid, g_lo] + [jnp.zeros_like(g_hi)] * 13)
    packed = jnp.concatenate(
        [s_chip.astype(BF16), jnp.broadcast_to(g_row[:, None], (16, n_state))], axis=0
    )
    everyone = lax.all_gather(packed, "ctx", axis=0, axis_index_groups=same_core)
    g_all = everyone[:, width : width + 3, 0].astype(F32)
    g_all = g_all[:, 0] + g_all[:, 1] + g_all[:, 2]
    at = jnp.arange(n_chip)
    between = (at[None, :] > at[:, None]) & (at[None, :] < chip)
    coef = jnp.prod(jnp.where(between, g_all[None, :], 1.0), axis=1)
    coef = jnp.where(at < chip, coef, 0.0)
    e0 = jnp.sum(coef[:, None, None] * everyone[:, :width].astype(F32), axis=0)
    e1 = g0 * e0 + s0
    kept = jnp.where(core == 0, e0, e1)
    came = swap_cores(jnp.where(core == 0, e1, e0), n_ctx)
    incoming = jnp.stack([jnp.where(core == 0, kept, came), jnp.where(core == 0, came, kept)])

    diagonal = jnp.einsum("hij,jhp->ihp", weights, values, preferred_element_type=F32)
    in_hi = incoming.astype(BF16)
    in_lo = (incoming - in_hi.astype(F32)).astype(BF16)
    offdiag = jnp.einsum("ni,hpn->ihp", c_t, in_hi, preferred_element_type=F32)
    offdiag = offdiag + jnp.einsum("ni,hpn->ihp", c_t, in_lo, preferred_element_type=F32)
    output = diagonal + offdiag * carry_in.T[:, :, None] + skip[None, :, None] * value_f
    gated = output * jax.nn.silu(gate.astype(F32))
    squares = jnp.sum(gated * gated, axis=(1, 2))
    squares = jnp.sum(to_all(squares, "fsdp"), axis=0)
    scale = lax.rsqrt(squares / (heads * width * n_fsdp) + 1e-05)
    return (gated * scale[:, None, None] * gain[None]).astype(BF16)


def solution(mesh):
    in_specs = (
        P("ctx", "fsdp"),
        P("ctx", "fsdp", None),
        P("ctx", None),
        P("fsdp", None),
        P("fsdp"),
        P("fsdp", "ctx"),
        P("ctx"),
    )
    out_specs = P("ctx", "fsdp", None)
    return jax.shard_map(
        per_device, mesh=mesh, in_specs=in_specs, out_specs=out_specs, check_vma=False
    )
```

```python
import functools

import jax
import jax.numpy as jnp
from jax import lax
from jax.experimental import pallas as pl
from jax.experimental.pallas import tpu as pltpu
from jax.sharding import PartitionSpec as P

F32 = jnp.float32
BF16 = jnp.bfloat16
PARAMS = pltpu.CompilerParams(vmem_limit_bytes=48 * 1024 * 1024)


def swap_cores(x):
    return lax.ppermute(x, "ctx", [(i, i ^ 1) for i in range(lax.axis_size("ctx"))])


def to_all(x, axis, groups=None):
    size = lax.axis_size(axis) if groups is None else len(groups[0])
    copies = jnp.broadcast_to(x[None], (size,) + x.shape)
    return lax.all_to_all(copies, axis, 0, 0, axis_index_groups=groups)


def maps_kernel(tok_ref, bc_ref, out_ref):
    acc = jnp.zeros(out_ref.shape, F32)
    for f in range(0, tok_ref.shape[0], 2):
        tok = jnp.concatenate([tok_ref[f], tok_ref[f + 1]], axis=1)
        bc = jnp.concatenate([bc_ref[f], bc_ref[f + 1]], axis=1)
        acc += lax.dot_general(bc, tok, (((1,), (1,)), ((), ())), preferred_element_type=F32)
    out_ref[...] = acc


def proj_kernel(n_w, tok_ref, *refs):
    out_ref = refs[-1]
    acc = jnp.zeros(out_ref.shape, F32)
    for f in range(0, tok_ref.shape[0], 2):
        tok = jnp.concatenate([tok_ref[f], tok_ref[f + 1]], axis=1)
        w = jnp.concatenate([r[g] for g in (f, f + 1) for r in refs[:n_w]], axis=0)
        acc += jnp.dot(tok, w, preferred_element_type=F32)
    out_ref[...] = acc


def project(tok, *ws):
    return pl.pallas_call(
        functools.partial(proj_kernel, len(ws)),
        out_shape=jax.ShapeDtypeStruct((tok.shape[1], ws[0].shape[2]), F32),
        compiler_params=PARAMS,
    )(tok, *ws)


def per_device(tokens, w_xz, w_bc, gain, skip, decays, boundaries):
    rows = tokens.shape[0]
    heads = w_xz.shape[1]
    width = w_xz.shape[2] // 2
    n_state = w_bc.shape[1] // 2
    n_ctx, n_fsdp = lax.axis_size("ctx"), lax.axis_size("fsdp")
    n_chip = n_ctx // 2
    ctx, fsdp = lax.axis_index("ctx"), lax.axis_index("fsdp")
    core, chip = ctx % 2, ctx // 2
    same_core = [[2 * z + c for z in range(n_chip)] for c in range(2)]
    depth = w_xz.shape[0]

    def mine_other(a, b):
        return jnp.where(core == 0, a, b), jnp.where(core == 0, b, a)

    w_gate = w_xz[:, :, width:].reshape(depth, -1)
    w_gate = lax.all_gather(w_gate, "ctx", axis=0, axis_index_groups=same_core)

    tok_mine, tok_other = mine_other(tokens[:, :depth], tokens[:, depth:])
    tok = jnp.concatenate([tok_mine, swap_cores(tok_other)], axis=0)
    tok = to_all(tok, "fsdp")

    share = w_bc.shape[1] // n_fsdp
    w_val = w_xz[:, :, :width].reshape(depth, -1)
    n_rest = 16
    bc_part = lax.dynamic_slice_in_dim(w_bc.T, fsdp * share, share, axis=0)
    rest = w_val[depth - n_rest :]
    small = jnp.concatenate([bc_part] + [rest[:, h * width : (h + 1) * width] for h in range(heads)])
    small = to_all(small, "ctx", same_core)
    bc_all = small[:, :share]
    rest_all = jnp.concatenate(
        [small[:, share + h * n_rest : share + (h + 1) * n_rest] for h in range(heads)], axis=2
    )
    w_val_all = lax.all_gather(
        w_val[: depth - n_rest], "ctx", axis=0, axis_index_groups=same_core
    )

    maps_t = pl.pallas_call(
        maps_kernel,
        out_shape=jax.ShapeDtypeStruct((share, 2 * rows), F32),
        compiler_params=PARAMS,
    )(tok, bc_all)
    maps_t = maps_t[:, :rows] + swap_cores(maps_t[:, rows:])
    maps_t = jax.nn.silu(maps_t).astype(BF16)
    maps_t = to_all(maps_t, "fsdp").reshape(2, n_state, rows)
    b_t, c_t = maps_t[0], maps_t[1]

    proj_v = project(tok, w_val_all, rest_all)
    proj_v = proj_v[:rows] + swap_cores(proj_v[rows:])
    values = jax.nn.silu(proj_v).astype(BF16).reshape(rows, heads, width)

    position = jnp.arange(rows)
    causal = position[:, None] >= position[None, :]
    cum = jnp.einsum(
        "hj,ij->hi", jnp.log(decays), causal.astype(F32), precision=lax.Precision.HIGHEST
    )
    seg = jnp.cumsum(boundaries)
    allowed = (seg[:, None] == seg[None, :]) & causal
    decay = jnp.where(allowed[None], jnp.exp(cum[:, :, None] - cum[:, None, :]), 0.0)
    scores = jnp.einsum("ni,nj->ij", c_t, b_t, preferred_element_type=F32)
    weights = (decay * scores[None]).astype(BF16)
    total, last = cum[:, -1], seg[-1]
    to_end = jnp.where((seg == last)[None], jnp.exp(total[:, None] - cum), 0.0)
    carry_in = jnp.where((seg == 0)[None], jnp.exp(cum), 0.0)
    gate_end = jnp.where(last == 0, jnp.exp(total), 0.0)

    value_f = values.astype(F32)
    scaled = (to_end.T[:, :, None] * value_f).astype(BF16)
    local = jnp.einsum("nj,jhp->hnp", b_t, scaled, preferred_element_type=F32)

    tail = jnp.broadcast_to(gate_end[:, None, None], (heads, 8, width))
    mine = jnp.concatenate([local, tail], axis=1)
    keep, send = mine_other(mine[0], mine[1])
    first, second = mine_other(keep, swap_cores(send))
    s0, g0, s1, g1 = first[:n_state], first[n_state, 0], second[:n_state], second[n_state, 0]
    s_chip, g_chip = g1 * s0 + s1, g0 * g1
    g_hi = g_chip.astype(BF16)
    g_mid = (g_chip - g_hi.astype(F32)).astype(BF16)
    g_lo = (g_chip - g_hi.astype(F32) - g_mid.astype(F32)).astype(BF16)
    g_row = jnp.stack([g_hi, g_mid, g_lo] + [jnp.zeros_like(g_hi)] * 13)
    packed = jnp.concatenate(
        [s_chip.astype(BF16), jnp.broadcast_to(g_row[:, None], (16, width))], axis=0
    )
    everyone = lax.all_gather(packed, "ctx", axis=0, axis_index_groups=same_core)
    g_all = everyone[:, n_state : n_state + 3, 0].astype(F32)
    g_all = g_all[:, 0] + g_all[:, 1] + g_all[:, 2]
    at = jnp.arange(n_chip)
    between = (at[None, :] > at[:, None]) & (at[None, :] < chip)
    coef = jnp.prod(jnp.where(between, g_all[None, :], 1.0), axis=1)
    coef = jnp.where(at < chip, coef, 0.0)
    e0 = jnp.sum(coef[:, None, None] * everyone[:, :n_state].astype(F32), axis=0)
    e1 = g0 * e0 + s0
    kept, give = mine_other(e0, e1)
    incoming = jnp.stack(mine_other(kept, swap_cores(give)))

    w_gate, tok, everyone = lax.optimization_barrier((w_gate, tok, everyone))
    proj_g = project(tok, w_gate)
    gate = (proj_g[:rows] + swap_cores(proj_g[rows:])).astype(BF16).reshape(rows, heads, width)

    diagonal = jnp.einsum("hij,jhp->ihp", weights, values, preferred_element_type=F32)
    in_hi = incoming.astype(BF16)
    in_lo = (incoming - in_hi.astype(F32)).astype(BF16)
    offdiag = jnp.einsum("ni,hnp->ihp", c_t, in_hi, preferred_element_type=F32)
    offdiag = offdiag + jnp.einsum("ni,hnp->ihp", c_t, in_lo, preferred_element_type=F32)
    output = diagonal + offdiag * carry_in.T[:, :, None] + skip[None, :, None] * value_f
    gated = output * jax.nn.silu(gate.astype(F32))
    squares = jnp.sum(gated * gated, axis=(1, 2))
    squares = jnp.sum(to_all(squares, "fsdp"), axis=0)
    scale = lax.rsqrt(squares / (heads * width * n_fsdp) + 1e-05)
    return (gated * scale[:, None, None] * gain[None]).astype(BF16)


def solution(mesh):
    in_specs = (
        P("ctx", "fsdp"),
        P("ctx", "fsdp", None),
        P("ctx", None),
        P("fsdp", None),
        P("fsdp"),
        P("fsdp", "ctx"),
        P("ctx"),
    )
    out_specs = P("ctx", "fsdp", None)
    return jax.shard_map(
        per_device, mesh=mesh, in_specs=in_specs, out_specs=out_specs, check_vma=False
    )
```

```python
import functools

import jax
import jax.numpy as jnp
from jax import lax
from jax.experimental import pallas as pl
from jax.experimental.pallas import tpu as pltpu
from jax.sharding import PartitionSpec as P

F32 = jnp.float32
BF16 = jnp.bfloat16
HIGH = lax.Precision.HIGHEST
PARAMS = pltpu.CompilerParams(vmem_limit_bytes=20 * 1024 * 1024)
NT = (((1,), (1,)), ((), ()))
TN = (((0,), (0,)), ((), ()))
VMEM = pl.BlockSpec(memory_space=pltpu.VMEM)
SMEM = pl.BlockSpec(memory_space=pltpu.SMEM)


def call(kernel, outs, *args, smem=0):
    shapes = [jax.ShapeDtypeStruct(s, t) for s, t in outs]
    got = pl.pallas_call(
        kernel,
        out_shape=shapes,
        in_specs=[SMEM] * smem + [VMEM] * (len(args) - smem),
        out_specs=[VMEM] * len(shapes),
        compiler_params=PARAMS,
    )(*args)
    return got[0] if len(shapes) == 1 else got


def silu(x):
    return x / (1.0 + jnp.exp(-x))


def shift(x, by):
    n = lax.axis_size("ctx")
    return lax.ppermute(x, "ctx", [(i, (i + by) % n) for i in range(n)])


def swap_cores(x):
    return lax.ppermute(x, "ctx", [(i, i ^ 1) for i in range(lax.axis_size("ctx"))])


def decay_kernel(decays_ref, starts_ref, cols_ref, decay_ref, ends_ref):
    heads, rows = decays_ref.shape
    i = lax.broadcasted_iota(jnp.int32, (rows, rows), 0)
    j = lax.broadcasted_iota(jnp.int32, (rows, rows), 1)
    causal = i >= j
    ones = causal.astype(F32)
    logs = jnp.log(decays_ref[...])
    starts = starts_ref[...].astype(F32)
    both = jnp.concatenate([logs, starts, jnp.zeros((8 - heads - 1, rows), F32)], axis=0)
    cum_row = lax.dot_general(both, ones, NT, precision=HIGH, preferred_element_type=F32)
    cum_col = lax.dot_general(ones, both, NT, precision=HIGH, preferred_element_type=F32)
    seg_row, seg_col = cum_row[heads : heads + 1], cum_col[:, heads : heads + 1]
    same = causal & (jnp.abs(seg_row - seg_col) < 0.5)
    last = cum_row[:, rows - 1 :]
    seg_last = last[heads : heads + 1]
    to_end, carry = [], []
    for h in range(heads):
        col = cum_col[:, h : h + 1]
        diff = col - cum_row[h : h + 1]
        decay_ref[h] = jnp.where(same, jnp.exp(diff), 0.0)
        total = last[h : h + 1]
        to_end.append(jnp.where(jnp.abs(seg_col - seg_last) < 0.5, jnp.exp(total - col), 0.0))
        carry.append(jnp.where(seg_col < 0.5, jnp.exp(col), 0.0))
        keep = jnp.where(seg_last < 0.5, jnp.exp(total), 0.0)
        ends_ref[h] = jnp.broadcast_to(keep, ends_ref.shape[1:])
    cols_ref[...] = jnp.concatenate(to_end + carry, axis=1)


def partial_kernel(steps, with_acc, chip_ref, tok_ref, *refs):
    n_out = 3
    blocks, outs = refs[: len(steps)], refs[-n_out:]
    n_chip, rows = tok_ref.shape[0], tok_ref.shape[1]
    half = rows // 2
    chip = chip_ref[0]
    edges = [0, outs[0].shape[1], outs[0].shape[1] + outs[2].shape[1]]
    if with_acc:
        acc = refs[len(steps)][...]
    else:
        acc = jnp.zeros((rows, edges[-1]), F32)
    order = list(zip(steps, blocks))
    for at in range(0, len(order), 2):
        part = order[at : at + 2]
        toks = [tok_ref[lax.rem(chip - s + 2 * n_chip, n_chip)] for s, _ in part]
        ws = [w[...] for _, w in part]
        tok = jnp.concatenate(toks, axis=1) if len(part) > 1 else toks[0]
        w = jnp.concatenate(ws, axis=0) if len(part) > 1 else ws[0]
        acc += jnp.dot(tok, w, preferred_element_type=F32)
    outs[0][...] = acc[:half, : edges[1]]
    outs[1][...] = acc[half:, : edges[1]]
    outs[2][...] = acc[:, edges[1] :]


def first_kernel(steps, chip_ref, tok_ref, *refs):
    blocks, out_ref = refs[: len(steps)], refs[-1]
    n_chip = tok_ref.shape[0]
    chip = chip_ref[0]
    acc = jnp.zeros(out_ref.shape, F32)
    order = list(zip(steps, blocks))
    for at in range(0, len(order), 2):
        part = order[at : at + 2]
        toks = [tok_ref[lax.rem(chip - s + 2 * n_chip, n_chip)] for s, _ in part]
        ws = [w[...] for _, w in part]
        tok = jnp.concatenate(toks, axis=1) if len(part) > 1 else toks[0]
        w = jnp.concatenate(ws, axis=0) if len(part) > 1 else ws[0]
        acc += jnp.dot(tok, w, preferred_element_type=F32)
    out_ref[...] = acc


def local_kernel(own_ref, got_ref, cols_ref, val_ref, maps_ref, local_ref):
    heads, n_state, width = local_ref.shape
    both = own_ref[...] + got_ref[...]
    act = silu(both).astype(BF16)
    values = act[:, : heads * width]
    maps = act[:, heads * width :]
    val_ref[...] = values
    maps_ref[...] = maps
    for h in range(heads):
        v = values[:, h * width : (h + 1) * width].astype(F32)
        scaled = (cols_ref[:, h : h + 1] * v).astype(BF16)
        local_ref[h] = lax.dot_general(maps[:, :n_state], scaled, TN, preferred_element_type=F32)


def diag_kernel(skip_ref, maps_ref, val_ref, decay_ref, out_ref):
    heads = decay_ref.shape[0]
    n_state = maps_ref.shape[1] // 2
    width = val_ref.shape[1] // heads
    scores = lax.dot_general(
        maps_ref[:, n_state:], maps_ref[:, :n_state], NT, preferred_element_type=F32
    )
    for h in range(heads):
        at = slice(h * width, (h + 1) * width)
        v = val_ref[:, at]
        weights = (decay_ref[h] * scores).astype(BF16)
        out = jnp.dot(weights, v, preferred_element_type=F32)
        out_ref[:, at] = out + skip_ref[h] * v.astype(F32)


def gated_kernel(heads, core_ref, diag_ref, kept_ref, came_ref, maps_ref, cols_ref, gate_ref, got_ref, out_ref, sum_ref):
    rows = diag_ref.shape[0]
    width = diag_ref.shape[1] // heads
    n_state = maps_ref.shape[1] // 2
    core = core_ref[0]
    c_map = maps_ref[:, n_state:]
    kept, came = kept_ref[...], came_ref[...]
    gate = (gate_ref[...] + got_ref[...]).astype(BF16).astype(F32)
    gate = silu(gate)
    total = jnp.zeros((rows, width), F32)
    for h in range(heads):
        at = slice(h * width, (h + 1) * width)
        state = jnp.where(core == h, kept, came)
        hi = state.astype(BF16)
        lo = (state - hi.astype(F32)).astype(BF16)
        off = jnp.dot(c_map, hi, preferred_element_type=F32)
        off += jnp.dot(c_map, lo, preferred_element_type=F32)
        out = diag_ref[:, at] + off * cols_ref[:, heads + h : heads + h + 1]
        gated = out * gate[:, at]
        out_ref[:, at] = gated
        total += gated * gated
    ones = jnp.ones((sum_ref.shape[0], width), F32)
    sum_ref[...] = lax.dot_general(ones, total, NT, precision=HIGH, preferred_element_type=F32)


def norm_kernel(count, sum_ref, gated_ref, gain_ref, out_ref):
    ones = jnp.ones((sum_ref.shape[0], gated_ref.shape[1]), F32)
    mean = lax.dot_general(sum_ref[...], ones, TN, precision=HIGH, preferred_element_type=F32)
    scale = lax.rsqrt(mean / count + 1e-05)
    out_ref[...] = (gated_ref[...] * scale * gain_ref[...]).astype(BF16)


def per_device(tokens, w_xz, w_bc, gain, skip, decays, boundaries):
    rows = tokens.shape[0]
    depth, heads = w_xz.shape[:2]
    width = w_xz.shape[2] // 2
    n_state = w_bc.shape[1] // 2
    n_ctx, n_fsdp = lax.axis_size("ctx"), lax.axis_size("fsdp")
    n_chip = n_ctx // 2
    ctx = lax.axis_index("ctx")
    core, chip = ctx % 2, ctx // 2
    same_core = [[2 * z + c for z in range(n_chip)] for c in range(2)]
    core_1, chip_1 = core.reshape(1), chip.reshape(1)

    def mine_other(a, b):
        return jnp.where(core == 0, a, b), jnp.where(core == 0, b, a)

    tok_mine, tok_other = mine_other(tokens[:, :depth], tokens[:, depth:])
    tok = jnp.concatenate([tok_mine, swap_cores(tok_other)], axis=0)
    copies = jnp.broadcast_to(tok[None], (n_fsdp,) + tok.shape)
    tok = lax.all_to_all(copies, "fsdp", 0, 0)

    block = jnp.concatenate(
        [w_xz[:, :, :width].reshape(depth, -1), w_bc, w_xz[:, :, width:].reshape(depth, -1)], axis=1
    )
    up = down = block
    steps, blocks = [0], [block]
    for s in range(1, n_chip // 2 + 1):
        up = shift(up, 2)
        steps.append(s)
        blocks.append(up)
        if s < n_chip // 2:
            down = shift(down, -2)
            steps.append(-s)
            blocks.append(down)
    early = n_chip - 4

    cols, decay, ends = call(
        decay_kernel,
        [((rows, 2 * heads), F32), ((heads, rows, rows), F32), ((heads, 8, width), F32)],
        decays,
        boundaries.reshape(1, rows),
    )

    n_first = heads * width + 2 * n_state
    acc = call(
        functools.partial(first_kernel, steps[:early]),
        [((2 * rows, block.shape[1]), F32)],
        chip_1,
        tok,
        *blocks[:early],
        smem=1,
    )
    own, other, gates = call(
        functools.partial(partial_kernel, steps[early:], True),
        [((rows, n_first), F32), ((rows, n_first), F32), ((2 * rows, heads * width), F32)],
        chip_1,
        tok,
        *blocks[early:],
        acc,
        smem=1,
    )
    got = swap_cores(other)
    gate_got = swap_cores(gates[rows:])
    values, maps, local = call(
        local_kernel,
        [((rows, heads * width), BF16), ((rows, 2 * n_state), BF16), ((heads, n_state, width), F32)],
        own,
        got,
        cols,
    )

    mine = jnp.concatenate([local, ends], axis=1)
    keep, send = mine_other(mine[0], mine[1])
    first, second = mine_other(keep, swap_cores(send))
    diag = call(diag_kernel, [((rows, heads * width), F32)], skip, maps, values, decay, smem=1)
    s0, g0, s1, g1 = first[:n_state], first[n_state, 0], second[:n_state], second[n_state, 0]
    s_chip, g_chip = g1 * s0 + s1, g0 * g1
    g_hi = g_chip.astype(BF16)
    g_mid = (g_chip - g_hi.astype(F32)).astype(BF16)
    g_lo = (g_chip - g_hi.astype(F32) - g_mid.astype(F32)).astype(BF16)
    g_row = jnp.stack([g_hi, g_mid, g_lo] + [jnp.zeros_like(g_hi)] * 13)
    packed = jnp.concatenate(
        [s_chip.astype(BF16), jnp.broadcast_to(g_row[:, None], (16, width))], axis=0
    )
    everyone = lax.all_gather(packed, "ctx", axis=0, axis_index_groups=same_core)
    g_all = everyone[:, n_state : n_state + 3, 0].astype(F32)
    g_all = g_all[:, 0] + g_all[:, 1] + g_all[:, 2]
    at = jnp.arange(n_chip)
    between = (at[None, :] > at[:, None]) & (at[None, :] < chip)
    coef = jnp.prod(jnp.where(between, g_all[None, :], 1.0), axis=1)
    coef = jnp.where(at < chip, coef, 0.0)
    e0 = jnp.sum(coef[:, None, None] * everyone[:, :n_state].astype(F32), axis=0)
    e1 = g0 * e0 + s0
    kept, give = mine_other(e0, e1)
    came = swap_cores(give)

    gated, sums = call(
        functools.partial(gated_kernel, heads),
        [((rows, heads * width), F32), ((n_fsdp, rows), F32)],
        core_1,
        diag,
        kept,
        came,
        maps,
        cols,
        gates[:rows],
        gate_got,
        smem=1,
    )
    sums = lax.all_to_all(sums, "fsdp", 0, 0, tiled=True)
    out = call(
        functools.partial(norm_kernel, heads * width * n_fsdp),
        [((rows, heads * width), BF16)],
        sums,
        gated,
        gain.reshape(1, -1),
    )
    return out.reshape(rows, heads, width)


def solution(mesh):
    in_specs = (
        P("ctx", "fsdp"),
        P("ctx", "fsdp", None),
        P("ctx", None),
        P("fsdp", None),
        P("fsdp"),
        P("fsdp", "ctx"),
        P("ctx"),
    )
    out_specs = P("ctx", "fsdp", None)
    return jax.shard_map(
        per_device, mesh=mesh, in_specs=in_specs, out_specs=out_specs, check_vma=False
    )
```

```python
import functools

import jax
import jax.numpy as jnp
from jax import lax
from jax.experimental import pallas as pl
from jax.experimental.pallas import tpu as pltpu
from jax.sharding import PartitionSpec as P

F32 = jnp.float32
BF16 = jnp.bfloat16
HIGH = lax.Precision.HIGHEST
PARAMS = pltpu.CompilerParams(vmem_limit_bytes=20 * 1024 * 1024)
NT = (((1,), (1,)), ((), ()))
TN = (((0,), (0,)), ((), ()))
VMEM = pl.BlockSpec(memory_space=pltpu.VMEM)
SMEM = pl.BlockSpec(memory_space=pltpu.SMEM)


def call(kernel, outs, *args, smem=0):
    shapes = [jax.ShapeDtypeStruct(s, t) for s, t in outs]
    got = pl.pallas_call(
        kernel,
        out_shape=shapes,
        in_specs=[SMEM] * smem + [VMEM] * (len(args) - smem),
        out_specs=[VMEM] * len(shapes),
        compiler_params=PARAMS,
    )(*args)
    return got[0] if len(shapes) == 1 else got


def silu(x):
    return x / (1.0 + jnp.exp(-x))


def shift(x, by):
    n = lax.axis_size("ctx")
    return lax.ppermute(x, "ctx", [(i, (i + by) % n) for i in range(n)])


def swap_cores(x):
    return lax.ppermute(x, "ctx", [(i, i ^ 1) for i in range(lax.axis_size("ctx"))])


def decay_kernel(decays_ref, starts_ref, cols_ref, decay_ref, ends_ref):
    heads, rows = decays_ref.shape
    i = lax.broadcasted_iota(jnp.int32, (rows, rows), 0)
    j = lax.broadcasted_iota(jnp.int32, (rows, rows), 1)
    causal = i >= j
    ones = causal.astype(F32)
    logs = jnp.log(decays_ref[...])
    starts = starts_ref[...].astype(F32)
    both = jnp.concatenate([logs, starts, jnp.zeros((8 - heads - 1, rows), F32)], axis=0)
    cum_row = lax.dot_general(both, ones, NT, precision=HIGH, preferred_element_type=F32)
    cum_col = lax.dot_general(ones, both, NT, precision=HIGH, preferred_element_type=F32)
    seg_row, seg_col = cum_row[heads : heads + 1], cum_col[:, heads : heads + 1]
    same = causal & (jnp.abs(seg_row - seg_col) < 0.5)
    last = cum_row[:, rows - 1 :]
    seg_last = last[heads : heads + 1]
    to_end, carry = [], []
    for h in range(heads):
        col = cum_col[:, h : h + 1]
        diff = col - cum_row[h : h + 1]
        decay_ref[h] = jnp.where(same, jnp.exp(diff), 0.0)
        total = last[h : h + 1]
        to_end.append(jnp.where(jnp.abs(seg_col - seg_last) < 0.5, jnp.exp(total - col), 0.0))
        carry.append(jnp.where(seg_col < 0.5, jnp.exp(col), 0.0))
        keep = jnp.where(seg_last < 0.5, jnp.exp(total), 0.0)
        ends_ref[h] = jnp.broadcast_to(keep, ends_ref.shape[1:])
    cols_ref[...] = jnp.concatenate(to_end + carry, axis=1)


def partial_kernel(steps, with_acc, chip_ref, tok_ref, *refs):
    count = len(steps)
    blocks, outs, held, sem = refs[:count], refs[count + with_acc : -2], refs[-2], refs[-1]
    copies = [
        pltpu.make_async_copy(block, held.at[at], sem.at[at]) for at, block in enumerate(blocks)
    ]
    for copy in copies:
        copy.start()
    n_chip, rows = tok_ref.shape[0], tok_ref.shape[1]
    chip = chip_ref[0]
    acc = refs[count][...] if with_acc else jnp.zeros((rows, held.shape[2]), F32)
    for at in range(0, count, 2):
        part = range(at, min(at + 2, count))
        for p in part:
            copies[p].wait()
        toks = [tok_ref[lax.rem(chip - steps[p] + 2 * n_chip, n_chip)] for p in part]
        ws = [held[p] for p in part]
        tok = jnp.concatenate(toks, axis=1) if len(part) > 1 else toks[0]
        w = jnp.concatenate(ws, axis=0) if len(part) > 1 else ws[0]
        acc += jnp.dot(tok, w, preferred_element_type=F32)
    if len(outs) == 1:
        outs[0][...] = acc
    else:
        outs[0][...] = acc[: rows // 2]
        outs[1][...] = acc[rows // 2 :]


def partial_product(n_out, steps, chip, tok, blocks, acc):
    shape = (tok.shape[1] // n_out, blocks[0].shape[1])
    count = len(steps)
    return pl.pallas_call(
        functools.partial(partial_kernel, steps, len(acc)),
        out_shape=[jax.ShapeDtypeStruct(shape, F32)] * n_out,
        in_specs=[SMEM, VMEM] + [pl.BlockSpec(memory_space=pltpu.HBM)] * count + [VMEM] * len(acc),
        out_specs=[VMEM] * n_out,
        scratch_shapes=[
            pltpu.VMEM((count,) + blocks[0].shape, BF16),
            pltpu.SemaphoreType.DMA((count,)),
        ],
        compiler_params=PARAMS,
    )(chip, tok, *blocks, *acc)


def local_kernel(core_ref, own_ref, got_ref, cols_ref, ends_ref, val_ref, maps_ref, keep_ref, send_ref):
    heads, spare, width = ends_ref.shape
    n_state = keep_ref.shape[0] - spare
    n_val = heads * width
    both = own_ref[:, : n_val + 2 * n_state] + got_ref[:, : n_val + 2 * n_state]
    act = silu(both).astype(BF16)
    values = act[:, :n_val]
    maps = act[:, n_val:]
    val_ref[...] = values
    maps_ref[...] = maps
    states = []
    for h in range(heads):
        v = values[:, h * width : (h + 1) * width].astype(F32)
        scaled = (cols_ref[:, h : h + 1] * v).astype(BF16)
        states.append(
            lax.dot_general(maps[:, :n_state], scaled, TN, preferred_element_type=F32)
        )
    even = core_ref[0] == 0
    keep_ref[:n_state] = jnp.where(even, states[0], states[1])
    send_ref[:n_state] = jnp.where(even, states[1], states[0])
    keep_ref[n_state:] = jnp.where(even, ends_ref[0], ends_ref[1])
    send_ref[n_state:] = jnp.where(even, ends_ref[1], ends_ref[0])


def chip_kernel(core_ref, keep_ref, got_ref, first_ref, packed_ref):
    spare = packed_ref.shape[0] - 16
    even = core_ref[0] == 0
    keep, got = keep_ref[...], got_ref[...]
    first, second = jnp.where(even, keep, got), jnp.where(even, got, keep)
    first_ref[...] = first
    s0, g0 = first[:spare], first[spare : spare + 1]
    s1, g1 = second[:spare], second[spare : spare + 1]
    packed_ref[:spare] = (g1 * s0 + s1).astype(BF16)
    gate = jnp.broadcast_to(g0 * g1, (16, s0.shape[1]))
    hi = gate.astype(BF16).astype(F32)
    mid = (gate - hi).astype(BF16).astype(F32)
    low = gate - hi - mid
    row = lax.broadcasted_iota(jnp.int32, gate.shape, 0)
    parts = jnp.where(row == 0, hi, jnp.where(row == 1, mid, jnp.where(row == 2, low, 0.0)))
    packed_ref[spare:] = parts.astype(BF16)


def incoming_kernel(core_ref, chip_ref, all_ref, first_ref, keep_ref, give_ref):
    n_chip, n_state = all_ref.shape[0], keep_ref.shape[0]
    chip = chip_ref[0]
    state = jnp.zeros(keep_ref.shape, F32)
    for z in range(n_chip - 1):
        parts = all_ref[z, n_state:].astype(F32)
        gate = parts[0:1] + parts[1:2] + parts[2:3]
        later = gate * state + all_ref[z, :n_state].astype(F32)
        state = jnp.where(z < chip, later, state)
    second = first_ref[n_state : n_state + 1] * state + first_ref[:n_state]
    even = core_ref[0] == 0
    keep_ref[...] = jnp.where(even, state, second)
    give_ref[...] = jnp.where(even, second, state)


def diag_kernel(skip_ref, maps_ref, val_ref, decay_ref, out_ref):
    heads = decay_ref.shape[0]
    n_state = maps_ref.shape[1] // 2
    width = val_ref.shape[1] // heads
    scores = lax.dot_general(
        maps_ref[:, n_state:], maps_ref[:, :n_state], NT, preferred_element_type=F32
    )
    for h in range(heads):
        at = slice(h * width, (h + 1) * width)
        v = val_ref[:, at]
        weights = (decay_ref[h] * scores).astype(BF16)
        out = jnp.dot(weights, v, preferred_element_type=F32)
        out_ref[:, at] = out + skip_ref[h] * v.astype(F32)


def gated_kernel(heads, core_ref, diag_ref, kept_ref, came_ref, maps_ref, cols_ref, gate_ref, got_ref, out_ref, sum_ref):
    rows = diag_ref.shape[0]
    width = diag_ref.shape[1] // heads
    n_state = maps_ref.shape[1] // 2
    core = core_ref[0]
    c_map = maps_ref[:, n_state:]
    kept, came = kept_ref[...], came_ref[...]
    n_gate = gate_ref.shape[1] - heads * width
    gate = (gate_ref[:, n_gate:] + got_ref[:, n_gate:]).astype(BF16).astype(F32)
    gate = silu(gate)
    total = jnp.zeros((rows, width), F32)
    for h in range(heads):
        at = slice(h * width, (h + 1) * width)
        state = jnp.where(core == h, kept, came)
        hi = state.astype(BF16)
        lo = (state - hi.astype(F32)).astype(BF16)
        off = jnp.dot(c_map, hi, preferred_element_type=F32)
        off += jnp.dot(c_map, lo, preferred_element_type=F32)
        out = diag_ref[:, at] + off * cols_ref[:, heads + h : heads + h + 1]
        gated = out * gate[:, at]
        out_ref[:, at] = gated
        total += gated * gated
    ones = jnp.ones((sum_ref.shape[0], width), F32)
    sum_ref[...] = lax.dot_general(ones, total, NT, precision=HIGH, preferred_element_type=F32)


def norm_kernel(count, sum_ref, gated_ref, gain_ref, out_ref):
    ones = jnp.ones((sum_ref.shape[0], gated_ref.shape[1]), F32)
    mean = lax.dot_general(sum_ref[...], ones, TN, precision=HIGH, preferred_element_type=F32)
    scale = lax.rsqrt(mean / count + 1e-05)
    out_ref[...] = (gated_ref[...] * scale * gain_ref[...]).astype(BF16)


def per_device(tokens, w_xz, w_bc, gain, skip, decays, boundaries):
    rows = tokens.shape[0]
    depth, heads = w_xz.shape[:2]
    width = w_xz.shape[2] // 2
    n_state = w_bc.shape[1] // 2
    n_ctx, n_fsdp = lax.axis_size("ctx"), lax.axis_size("fsdp")
    n_chip = n_ctx // 2
    ctx = lax.axis_index("ctx")
    core, chip = ctx % 2, ctx // 2
    same_core = [[2 * z + c for z in range(n_chip)] for c in range(2)]
    core_1, chip_1 = core.reshape(1), chip.reshape(1)

    def mine_other(a, b):
        return jnp.where(core == 0, a, b), jnp.where(core == 0, b, a)

    tok_mine, tok_other = mine_other(tokens[:, :depth], tokens[:, depth:])
    tok = jnp.concatenate([tok_mine, swap_cores(tok_other)], axis=0)
    copies = jnp.broadcast_to(tok[None], (n_fsdp,) + tok.shape)
    tok = lax.all_to_all(copies, "fsdp", 0, 0)

    block = jnp.concatenate(
        [w_xz[:, :, :width].reshape(depth, -1), w_bc, w_xz[:, :, width:].reshape(depth, -1)], axis=1
    )
    n_val = heads * width
    cols, decay, ends = call(
        decay_kernel,
        [((rows, 2 * heads), F32), ((heads, rows, rows), F32), ((heads, 8, width), F32)],
        decays,
        boundaries.reshape(1, rows),
    )
    up = down = block
    steps, blocks, acc = [0], [block], ()
    half = n_chip // 2
    for s in range(1, half + 1):
        if s in (half - 2, half):
            product = partial_product(1, steps, chip_1, tok, blocks, acc)[0]
            up, down, product, cols, decay, ends = lax.optimization_barrier(
                (up, down, product, cols, decay, ends)
            )
            steps, blocks, acc = [], [], (product,)
        up = shift(up, 2)
        steps.append(s)
        blocks.append(up)
        if s < half:
            down = shift(down, -2)
            steps.append(-s)
            blocks.append(down)
    own, other = partial_product(2, steps, chip_1, tok, blocks, acc)
    got = swap_cores(other)

    state = ((n_state + 8, width), F32)
    values, maps, keep, send = call(
        local_kernel,
        [((rows, n_val), BF16), ((rows, 2 * n_state), BF16), state, state],
        core_1,
        own,
        got,
        cols,
        ends,
        smem=1,
    )
    came = swap_cores(send)
    diag = call(diag_kernel, [((rows, n_val), F32)], skip, maps, values, decay, smem=1)
    first, packed = call(
        chip_kernel, [state, ((n_state + 16, width), BF16)], core_1, keep, came, smem=1
    )
    everyone = lax.all_gather(packed, "ctx", axis=0, axis_index_groups=same_core)
    kept, give = call(
        incoming_kernel,
        [((n_state, width), F32)] * 2,
        core_1,
        chip_1,
        everyone,
        first,
        smem=2,
    )
    came = swap_cores(give)

    gated, sums = call(
        functools.partial(gated_kernel, heads),
        [((rows, heads * width), F32), ((n_fsdp, rows), F32)],
        core_1,
        diag,
        kept,
        came,
        maps,
        cols,
        own,
        got,
        smem=1,
    )
    sums = lax.all_to_all(sums, "fsdp", 0, 0, tiled=True)
    out = call(
        functools.partial(norm_kernel, heads * width * n_fsdp),
        [((rows, heads * width), BF16)],
        sums,
        gated,
        gain.reshape(1, -1),
    )
    return out.reshape(rows, heads, width)


def solution(mesh):
    in_specs = (
        P("ctx", "fsdp"),
        P("ctx", "fsdp", None),
        P("ctx", None),
        P("fsdp", None),
        P("fsdp"),
        P("fsdp", "ctx"),
        P("ctx"),
    )
    out_specs = P("ctx", "fsdp", None)
    return jax.shard_map(
        per_device, mesh=mesh, in_specs=in_specs, out_specs=out_specs, check_vma=False
    )
```

```python
import functools

import jax
import jax.numpy as jnp
from jax import lax
from jax.experimental import pallas as pl
from jax.experimental.pallas import tpu as pltpu
from jax.sharding import PartitionSpec as P

F32 = jnp.float32
BF16 = jnp.bfloat16
HIGH = lax.Precision.HIGHEST
PARAMS = pltpu.CompilerParams(vmem_limit_bytes=20 * 1024 * 1024)
NT = (((1,), (1,)), ((), ()))
TN = (((0,), (0,)), ((), ()))
VMEM = pl.BlockSpec(memory_space=pltpu.VMEM)
SMEM = pl.BlockSpec(memory_space=pltpu.SMEM)


def call(kernel, outs, *args, smem=0):
    shapes = [jax.ShapeDtypeStruct(s, t) for s, t in outs]
    got = pl.pallas_call(
        kernel,
        out_shape=shapes,
        in_specs=[SMEM] * smem + [VMEM] * (len(args) - smem),
        out_specs=[VMEM] * len(shapes),
        compiler_params=PARAMS,
    )(*args)
    return got[0] if len(shapes) == 1 else got


def silu(x):
    return x / (1.0 + jnp.exp(-x))


def shift(x, by):
    n = lax.axis_size("ctx")
    return lax.ppermute(x, "ctx", [(i, (i + by) % n) for i in range(n)])


def swap_cores(x):
    return lax.ppermute(x, "ctx", [(i, i ^ 1) for i in range(lax.axis_size("ctx"))])


def decay_kernel(decays_ref, starts_ref, cols_ref, decay_ref, ends_ref):
    heads, rows = decays_ref.shape
    i = lax.broadcasted_iota(jnp.int32, (rows, rows), 0)
    j = lax.broadcasted_iota(jnp.int32, (rows, rows), 1)
    causal = i >= j
    ones = causal.astype(F32)
    logs = jnp.log(decays_ref[...])
    starts = starts_ref[...].astype(F32)
    both = jnp.concatenate([logs, starts, jnp.zeros((8 - heads - 1, rows), F32)], axis=0)
    cum_row = lax.dot_general(both, ones, NT, precision=HIGH, preferred_element_type=F32)
    cum_col = lax.dot_general(ones, both, NT, precision=HIGH, preferred_element_type=F32)
    seg_row, seg_col = cum_row[heads : heads + 1], cum_col[:, heads : heads + 1]
    same = causal & (jnp.abs(seg_row - seg_col) < 0.5)
    last = cum_row[:, rows - 1 :]
    seg_last = last[heads : heads + 1]
    to_end, carry = [], []
    for h in range(heads):
        col = cum_col[:, h : h + 1]
        diff = col - cum_row[h : h + 1]
        decay_ref[h] = jnp.where(same, jnp.exp(diff), 0.0)
        total = last[h : h + 1]
        to_end.append(jnp.where(jnp.abs(seg_col - seg_last) < 0.5, jnp.exp(total - col), 0.0))
        carry.append(jnp.where(seg_col < 0.5, jnp.exp(col), 0.0))
        keep = jnp.where(seg_last < 0.5, jnp.exp(total), 0.0)
        ends_ref[h] = jnp.broadcast_to(keep, ends_ref.shape[1:])
    cols_ref[...] = jnp.concatenate(to_end + carry, axis=1)


def partial_kernel(steps, with_acc, chip_ref, tok_ref, *refs):
    blocks, outs = refs[: len(steps)], refs[len(steps) + with_acc :]
    n_chip, rows = tok_ref.shape[0], tok_ref.shape[1]
    chip = chip_ref[0]
    acc = refs[len(steps)][...] if with_acc else jnp.zeros((rows, blocks[0].shape[1]), F32)
    order = list(zip(steps, blocks))
    for at in range(0, len(order), 2):
        part = order[at : at + 2]
        toks = [tok_ref[lax.rem(chip - s + 2 * n_chip, n_chip)] for s, _ in part]
        ws = [w[...] for _, w in part]
        tok = jnp.concatenate(toks, axis=1) if len(part) > 1 else toks[0]
        w = jnp.concatenate(ws, axis=0) if len(part) > 1 else ws[0]
        acc += jnp.dot(tok, w, preferred_element_type=F32)
    if len(outs) == 1:
        outs[0][...] = acc
    else:
        outs[0][...] = acc[: rows // 2]
        outs[1][...] = acc[rows // 2 :]


def partial_product(n_out, steps, chip, tok, blocks, acc):
    shape = (tok.shape[1] // n_out, blocks[0].shape[1])
    got = call(
        functools.partial(partial_kernel, steps, len(acc)),
        [(shape, F32)] * n_out,
        chip,
        tok,
        *blocks,
        *acc,
        smem=1,
    )
    return [got] if n_out == 1 else got


def local_kernel(core_ref, own_ref, got_ref, cols_ref, ends_ref, val_ref, maps_ref, keep_ref, send_ref):
    heads, spare, width = ends_ref.shape
    n_state = keep_ref.shape[0] - spare
    n_val = heads * width
    both = own_ref[:, : n_val + 2 * n_state] + got_ref[:, : n_val + 2 * n_state]
    act = silu(both).astype(BF16)
    values = act[:, :n_val]
    maps = act[:, n_val:]
    val_ref[...] = values
    maps_ref[...] = maps
    states = []
    for h in range(heads):
        v = values[:, h * width : (h + 1) * width].astype(F32)
        scaled = (cols_ref[:, h : h + 1] * v).astype(BF16)
        states.append(
            lax.dot_general(maps[:, :n_state], scaled, TN, preferred_element_type=F32)
        )
    even = core_ref[0] == 0
    keep_ref[:n_state] = jnp.where(even, states[0], states[1])
    send_ref[:n_state] = jnp.where(even, states[1], states[0])
    keep_ref[n_state:] = jnp.where(even, ends_ref[0], ends_ref[1])
    send_ref[n_state:] = jnp.where(even, ends_ref[1], ends_ref[0])


def chip_kernel(core_ref, keep_ref, got_ref, first_ref, packed_ref):
    spare = packed_ref.shape[0] - 16
    even = core_ref[0] == 0
    keep, got = keep_ref[...], got_ref[...]
    first, second = jnp.where(even, keep, got), jnp.where(even, got, keep)
    first_ref[...] = first
    s0, g0 = first[:spare], first[spare : spare + 1]
    s1, g1 = second[:spare], second[spare : spare + 1]
    packed_ref[:spare] = (g1 * s0 + s1).astype(BF16)
    gate = jnp.broadcast_to(g0 * g1, (16, s0.shape[1]))
    hi = gate.astype(BF16).astype(F32)
    mid = (gate - hi).astype(BF16).astype(F32)
    low = gate - hi - mid
    row = lax.broadcasted_iota(jnp.int32, gate.shape, 0)
    parts = jnp.where(row == 0, hi, jnp.where(row == 1, mid, jnp.where(row == 2, low, 0.0)))
    packed_ref[spare:] = parts.astype(BF16)


def incoming_kernel(core_ref, chip_ref, all_ref, first_ref, keep_ref, give_ref):
    n_chip, n_state = all_ref.shape[0], keep_ref.shape[0]
    chip = chip_ref[0]
    state = jnp.zeros(keep_ref.shape, F32)
    for z in range(n_chip - 1):
        parts = all_ref[z, n_state:].astype(F32)
        gate = parts[0:1] + parts[1:2] + parts[2:3]
        later = gate * state + all_ref[z, :n_state].astype(F32)
        state = jnp.where(z < chip, later, state)
    second = first_ref[n_state : n_state + 1] * state + first_ref[:n_state]
    even = core_ref[0] == 0
    keep_ref[...] = jnp.where(even, state, second)
    give_ref[...] = jnp.where(even, second, state)


def diag_kernel(skip_ref, maps_ref, val_ref, decay_ref, out_ref):
    heads = decay_ref.shape[0]
    n_state = maps_ref.shape[1] // 2
    width = val_ref.shape[1] // heads
    scores = lax.dot_general(
        maps_ref[:, n_state:], maps_ref[:, :n_state], NT, preferred_element_type=F32
    )
    for h in range(heads):
        at = slice(h * width, (h + 1) * width)
        v = val_ref[:, at]
        weights = (decay_ref[h] * scores).astype(BF16)
        out = jnp.dot(weights, v, preferred_element_type=F32)
        out_ref[:, at] = out + skip_ref[h] * v.astype(F32)


def gated_kernel(heads, core_ref, diag_ref, kept_ref, came_ref, maps_ref, cols_ref, gate_ref, got_ref, out_ref, sum_ref):
    rows = diag_ref.shape[0]
    width = diag_ref.shape[1] // heads
    n_state = maps_ref.shape[1] // 2
    core = core_ref[0]
    c_map = maps_ref[:, n_state:]
    kept, came = kept_ref[...], came_ref[...]
    n_gate = gate_ref.shape[1] - heads * width
    gate = (gate_ref[:, n_gate:] + got_ref[:, n_gate:]).astype(BF16).astype(F32)
    gate = silu(gate)
    total = jnp.zeros((rows, width), F32)
    for h in range(heads):
        at = slice(h * width, (h + 1) * width)
        state = jnp.where(core == h, kept, came)
        hi = state.astype(BF16)
        lo = (state - hi.astype(F32)).astype(BF16)
        off = jnp.dot(c_map, hi, preferred_element_type=F32)
        off += jnp.dot(c_map, lo, preferred_element_type=F32)
        out = diag_ref[:, at] + off * cols_ref[:, heads + h : heads + h + 1]
        gated = out * gate[:, at]
        out_ref[:, at] = gated
        total += gated * gated
    ones = jnp.ones((sum_ref.shape[0], width), F32)
    sum_ref[...] = lax.dot_general(ones, total, NT, precision=HIGH, preferred_element_type=F32)


def norm_kernel(count, sum_ref, gated_ref, gain_ref, out_ref):
    ones = jnp.ones((sum_ref.shape[0], gated_ref.shape[1]), F32)
    mean = lax.dot_general(sum_ref[...], ones, TN, precision=HIGH, preferred_element_type=F32)
    scale = lax.rsqrt(mean / count + 1e-05)
    out_ref[...] = (gated_ref[...] * scale * gain_ref[...]).astype(BF16)


def per_device(tokens, w_xz, w_bc, gain, skip, decays, boundaries):
    rows = tokens.shape[0]
    depth, heads = w_xz.shape[:2]
    width = w_xz.shape[2] // 2
    n_state = w_bc.shape[1] // 2
    n_ctx, n_fsdp = lax.axis_size("ctx"), lax.axis_size("fsdp")
    n_chip = n_ctx // 2
    ctx = lax.axis_index("ctx")
    core, chip = ctx % 2, ctx // 2
    same_core = [[2 * z + c for z in range(n_chip)] for c in range(2)]
    core_1, chip_1 = core.reshape(1), chip.reshape(1)

    def mine_other(a, b):
        return jnp.where(core == 0, a, b), jnp.where(core == 0, b, a)

    block = jnp.concatenate(
        [w_xz[:, :, :width].reshape(depth, -1), w_bc, w_xz[:, :, width:].reshape(depth, -1)], axis=1
    )
    n_val = heads * width
    cols, decay, ends = call(
        decay_kernel,
        [((rows, 2 * heads), F32), ((heads, rows, rows), F32), ((heads, 8, width), F32)],
        decays,
        boundaries.reshape(1, rows),
    )
    half = n_chip // 2
    early = half - 3
    up = down = block
    steps, blocks, acc = [0], [block], ()
    for s in range(1, half + 1):
        if s == half:
            up, product, cols, decay, ends = lax.optimization_barrier(
                (up, product, cols, decay, ends)
            )
            acc = (product,)
        up = shift(up, 2)
        steps.append(s)
        blocks.append(up)
        if s < half:
            down = shift(down, -2)
            steps.append(-s)
            blocks.append(down)
        if s == 1:
            up, tokens = lax.optimization_barrier((up, tokens))
            tok_mine, tok_other = mine_other(tokens[:, :depth], tokens[:, depth:])
            tok = jnp.concatenate([tok_mine, swap_cores(tok_other)], axis=0)
            copies = jnp.broadcast_to(tok[None], (n_fsdp,) + tok.shape)
            tok = lax.all_to_all(copies, "fsdp", 0, 0)
        if s == early:
            product = partial_product(1, steps, chip_1, tok, blocks, acc)[0]
            steps, blocks = [], []
    own, other = partial_product(2, steps, chip_1, tok, blocks, acc)
    got = swap_cores(other)

    state = ((n_state + 8, width), F32)
    values, maps, keep, send = call(
        local_kernel,
        [((rows, n_val), BF16), ((rows, 2 * n_state), BF16), state, state],
        core_1,
        own,
        got,
        cols,
        ends,
        smem=1,
    )
    came = swap_cores(send)
    diag = call(diag_kernel, [((rows, n_val), F32)], skip, maps, values, decay, smem=1)
    first, packed = call(
        chip_kernel, [state, ((n_state + 16, width), BF16)], core_1, keep, came, smem=1
    )
    everyone = lax.all_gather(packed, "ctx", axis=0, axis_index_groups=same_core)
    kept, give = call(
        incoming_kernel,
        [((n_state, width), F32)] * 2,
        core_1,
        chip_1,
        everyone,
        first,
        smem=2,
    )
    came = swap_cores(give)

    gated, sums = call(
        functools.partial(gated_kernel, heads),
        [((rows, heads * width), F32), ((n_fsdp, rows), F32)],
        core_1,
        diag,
        kept,
        came,
        maps,
        cols,
        own,
        got,
        smem=1,
    )
    sums = lax.all_to_all(sums, "fsdp", 0, 0, tiled=True)
    out = call(
        functools.partial(norm_kernel, heads * width * n_fsdp),
        [((rows, heads * width), BF16)],
        sums,
        gated,
        gain.reshape(1, -1),
    )
    return out.reshape(rows, heads, width)


def solution(mesh):
    in_specs = (
        P("ctx", "fsdp"),
        P("ctx", "fsdp", None),
        P("ctx", None),
        P("fsdp", None),
        P("fsdp"),
        P("fsdp", "ctx"),
        P("ctx"),
    )
    out_specs = P("ctx", "fsdp", None)
    return jax.shard_map(
        per_device, mesh=mesh, in_specs=in_specs, out_specs=out_specs, check_vma=False
    )
```

```python
import functools

import jax
import jax.numpy as jnp
from jax import lax
from jax.experimental import pallas as pl
from jax.experimental.pallas import tpu as pltpu
from jax.sharding import PartitionSpec as P

F32 = jnp.float32
BF16 = jnp.bfloat16
HIGH = lax.Precision.HIGHEST
PARAMS = pltpu.CompilerParams(vmem_limit_bytes=20 * 1024 * 1024)
NT = (((1,), (1,)), ((), ()))
TN = (((0,), (0,)), ((), ()))
VMEM = pl.BlockSpec(memory_space=pltpu.VMEM)
SMEM = pl.BlockSpec(memory_space=pltpu.SMEM)


def call(kernel, outs, *args, smem=0):
    shapes = [jax.ShapeDtypeStruct(s, t) for s, t in outs]
    got = pl.pallas_call(
        kernel,
        out_shape=shapes,
        in_specs=[SMEM] * smem + [VMEM] * (len(args) - smem),
        out_specs=[VMEM] * len(shapes),
        compiler_params=PARAMS,
    )(*args)
    return got[0] if len(shapes) == 1 else got


def silu(x):
    return x / (1.0 + jnp.exp(-x))


def shift(x, by):
    n = lax.axis_size("ctx")
    return lax.ppermute(x, "ctx", [(i, (i + by) % n) for i in range(n)])


def swap_cores(x):
    return lax.ppermute(x, "ctx", [(i, i ^ 1) for i in range(lax.axis_size("ctx"))])


def decay_kernel(decays_ref, starts_ref, cols_ref, decay_ref, ends_ref):
    heads, rows = decays_ref.shape
    i = lax.broadcasted_iota(jnp.int32, (rows, rows), 0)
    j = lax.broadcasted_iota(jnp.int32, (rows, rows), 1)
    causal = i >= j
    ones = causal.astype(F32)
    logs = jnp.log(decays_ref[...])
    starts = starts_ref[...].astype(F32)
    both = jnp.concatenate([logs, starts, jnp.zeros((8 - heads - 1, rows), F32)], axis=0)
    cum_row = lax.dot_general(both, ones, NT, precision=HIGH, preferred_element_type=F32)
    cum_col = lax.dot_general(ones, both, NT, precision=HIGH, preferred_element_type=F32)
    seg_row, seg_col = cum_row[heads : heads + 1], cum_col[:, heads : heads + 1]
    same = causal & (jnp.abs(seg_row - seg_col) < 0.5)
    last = cum_row[:, rows - 1 :]
    seg_last = last[heads : heads + 1]
    to_end, carry = [], []
    for h in range(heads):
        col = cum_col[:, h : h + 1]
        diff = col - cum_row[h : h + 1]
        decay_ref[h] = jnp.where(same, jnp.exp(diff), 0.0)
        total = last[h : h + 1]
        to_end.append(jnp.where(jnp.abs(seg_col - seg_last) < 0.5, jnp.exp(total - col), 0.0))
        carry.append(jnp.where(seg_col < 0.5, jnp.exp(col), 0.0))
        keep = jnp.where(seg_last < 0.5, jnp.exp(total), 0.0)
        ends_ref[h] = jnp.broadcast_to(keep, ends_ref.shape[1:])
    cols_ref[...] = jnp.concatenate(to_end + carry, axis=1)


def partial_kernel(steps, with_acc, chip_ref, tok_ref, *refs):
    blocks, outs = refs[: len(steps)], refs[len(steps) + with_acc :]
    n_chip, rows = tok_ref.shape[0], tok_ref.shape[1]
    chip = chip_ref[0]
    acc = refs[len(steps)][...] if with_acc else jnp.zeros((rows, blocks[0].shape[1]), F32)
    order = list(zip(steps, blocks))
    for at in range(0, len(order), 2):
        part = order[at : at + 2]
        toks = [tok_ref[lax.rem(chip - s + 2 * n_chip, n_chip)] for s, _ in part]
        ws = [w[...] for _, w in part]
        tok = jnp.concatenate(toks, axis=1) if len(part) > 1 else toks[0]
        w = jnp.concatenate(ws, axis=0) if len(part) > 1 else ws[0]
        acc += jnp.dot(tok, w, preferred_element_type=F32)
    if len(outs) == 1:
        outs[0][...] = acc
    else:
        outs[0][...] = acc[: rows // 2]
        outs[1][...] = acc[rows // 2 :]


def partial_product(n_out, steps, chip, tok, blocks, acc):
    shape = (tok.shape[1] // n_out, blocks[0].shape[1])
    got = call(
        functools.partial(partial_kernel, steps, len(acc)),
        [(shape, F32)] * n_out,
        chip,
        tok,
        *blocks,
        *acc,
        smem=1,
    )
    return [got] if n_out == 1 else got


def local_kernel(core_ref, own_ref, got_ref, cols_ref, ends_ref, val_ref, maps_ref, keep_ref, send_ref):
    heads, spare, width = ends_ref.shape
    n_state = keep_ref.shape[0] - spare
    n_val = heads * width
    both = own_ref[:, : n_val + 2 * n_state] + got_ref[:, : n_val + 2 * n_state]
    act = silu(both).astype(BF16)
    values = act[:, :n_val]
    maps = act[:, n_val:]
    val_ref[...] = values
    maps_ref[...] = maps
    states = []
    for h in range(heads):
        v = values[:, h * width : (h + 1) * width].astype(F32)
        scaled = (cols_ref[:, h : h + 1] * v).astype(BF16)
        states.append(
            lax.dot_general(maps[:, :n_state], scaled, TN, preferred_element_type=F32)
        )
    even = core_ref[0] == 0
    keep_ref[:n_state] = jnp.where(even, states[0], states[1])
    send_ref[:n_state] = jnp.where(even, states[1], states[0])
    keep_ref[n_state:] = jnp.where(even, ends_ref[0], ends_ref[1])
    send_ref[n_state:] = jnp.where(even, ends_ref[1], ends_ref[0])


def chip_kernel(core_ref, keep_ref, got_ref, first_ref, packed_ref):
    spare = packed_ref.shape[0] - 16
    even = core_ref[0] == 0
    keep, got = keep_ref[...], got_ref[...]
    first, second = jnp.where(even, keep, got), jnp.where(even, got, keep)
    first_ref[...] = first
    s0, g0 = first[:spare], first[spare : spare + 1]
    s1, g1 = second[:spare], second[spare : spare + 1]
    packed_ref[:spare] = (g1 * s0 + s1).astype(BF16)
    gate = jnp.broadcast_to(g0 * g1, (16, s0.shape[1]))
    hi = gate.astype(BF16).astype(F32)
    mid = (gate - hi).astype(BF16).astype(F32)
    low = gate - hi - mid
    row = lax.broadcasted_iota(jnp.int32, gate.shape, 0)
    parts = jnp.where(row == 0, hi, jnp.where(row == 1, mid, jnp.where(row == 2, low, 0.0)))
    packed_ref[spare:] = parts.astype(BF16)


def incoming_kernel(core_ref, chip_ref, all_ref, first_ref, keep_ref, give_ref):
    n_chip, n_state = all_ref.shape[0], keep_ref.shape[0]
    chip = chip_ref[0]
    state = jnp.zeros(keep_ref.shape, F32)
    for z in range(n_chip - 1):
        parts = all_ref[z, n_state:].astype(F32)
        gate = parts[0:1] + parts[1:2] + parts[2:3]
        later = gate * state + all_ref[z, :n_state].astype(F32)
        state = jnp.where(z < chip, later, state)
    second = first_ref[n_state : n_state + 1] * state + first_ref[:n_state]
    even = core_ref[0] == 0
    keep_ref[...] = jnp.where(even, state, second)
    give_ref[...] = jnp.where(even, second, state)


def diag_kernel(skip_ref, maps_ref, val_ref, decay_ref, out_ref):
    heads = decay_ref.shape[0]
    n_state = maps_ref.shape[1] // 2
    width = val_ref.shape[1] // heads
    scores = lax.dot_general(
        maps_ref[:, n_state:], maps_ref[:, :n_state], NT, preferred_element_type=F32
    )
    for h in range(heads):
        at = slice(h * width, (h + 1) * width)
        v = val_ref[:, at]
        weights = (decay_ref[h] * scores).astype(BF16)
        out = jnp.dot(weights, v, preferred_element_type=F32)
        out_ref[:, at] = out + skip_ref[h] * v.astype(F32)


def gated_kernel(heads, core_ref, diag_ref, kept_ref, came_ref, maps_ref, cols_ref, gate_ref, got_ref, out_ref, sum_ref):
    rows = diag_ref.shape[0]
    width = diag_ref.shape[1] // heads
    n_state = maps_ref.shape[1] // 2
    core = core_ref[0]
    c_map = maps_ref[:, n_state:]
    kept, came = kept_ref[...], came_ref[...]
    n_gate = gate_ref.shape[1] - heads * width
    gate = (gate_ref[:, n_gate:] + got_ref[:, n_gate:]).astype(BF16).astype(F32)
    gate = silu(gate)
    total = jnp.zeros((rows, width), F32)
    for h in range(heads):
        at = slice(h * width, (h + 1) * width)
        state = jnp.where(core == h, kept, came)
        hi = state.astype(BF16)
        lo = (state - hi.astype(F32)).astype(BF16)
        off = jnp.dot(c_map, hi, preferred_element_type=F32)
        off += jnp.dot(c_map, lo, preferred_element_type=F32)
        out = diag_ref[:, at] + off * cols_ref[:, heads + h : heads + h + 1]
        gated = out * gate[:, at]
        out_ref[:, at] = gated
        total += gated * gated
    ones = jnp.ones((sum_ref.shape[0], width), F32)
    sum_ref[...] = lax.dot_general(ones, total, NT, precision=HIGH, preferred_element_type=F32)


def norm_kernel(count, sum_ref, gated_ref, gain_ref, out_ref):
    ones = jnp.ones((sum_ref.shape[0], gated_ref.shape[1]), F32)
    mean = lax.dot_general(sum_ref[...], ones, TN, precision=HIGH, preferred_element_type=F32)
    scale = lax.rsqrt(mean / count + 1e-05)
    out_ref[...] = (gated_ref[...] * scale * gain_ref[...]).astype(BF16)


def per_device(tokens, w_xz, w_bc, gain, skip, decays, boundaries):
    rows = tokens.shape[0]
    depth, heads = w_xz.shape[:2]
    width = w_xz.shape[2] // 2
    n_state = w_bc.shape[1] // 2
    n_ctx, n_fsdp = lax.axis_size("ctx"), lax.axis_size("fsdp")
    n_chip = n_ctx // 2
    ctx = lax.axis_index("ctx")
    core, chip = ctx % 2, ctx // 2
    same_core = [[2 * z + c for z in range(n_chip)] for c in range(2)]
    core_1, chip_1 = core.reshape(1), chip.reshape(1)

    def mine_other(a, b):
        return jnp.where(core == 0, a, b), jnp.where(core == 0, b, a)

    tok_mine, tok_other = mine_other(tokens[:, :depth], tokens[:, depth:])
    tok = jnp.concatenate([tok_mine, swap_cores(tok_other)], axis=0)
    copies = jnp.broadcast_to(tok[None], (n_fsdp,) + tok.shape)
    tok = lax.all_to_all(copies, "fsdp", 0, 0)

    block = jnp.concatenate(
        [w_xz[:, :, :width].reshape(depth, -1), w_bc, w_xz[:, :, width:].reshape(depth, -1)], axis=1
    )
    n_val = heads * width
    cols, decay, ends = call(
        decay_kernel,
        [((rows, 2 * heads), F32), ((heads, rows, rows), F32), ((heads, 8, width), F32)],
        decays,
        boundaries.reshape(1, rows),
    )
    half = n_chip // 2
    up = down = block
    steps, blocks, acc = [0], [block], ()
    for s in range(1, half + 1):
        up = shift(up, 2)
        steps.append(s)
        blocks.append(up)
        if s == half - 2:
            acc = partial_product(1, steps, chip_1, tok, blocks, acc)
            steps, blocks = [], []
        if s < half:
            down = shift(down, -2)
            steps.append(-s)
            blocks.append(down)
    own, other = partial_product(2, steps, chip_1, tok, blocks, acc)
    got = swap_cores(other)

    state = ((n_state + 8, width), F32)
    values, maps, keep, send = call(
        local_kernel,
        [((rows, n_val), BF16), ((rows, 2 * n_state), BF16), state, state],
        core_1,
        own,
        got,
        cols,
        ends,
        smem=1,
    )
    came = swap_cores(send)
    diag = call(diag_kernel, [((rows, n_val), F32)], skip, maps, values, decay, smem=1)
    first, packed = call(
        chip_kernel, [state, ((n_state + 16, width), BF16)], core_1, keep, came, smem=1
    )
    everyone = lax.all_gather(packed, "ctx", axis=0, axis_index_groups=same_core)
    kept, give = call(
        incoming_kernel,
        [((n_state, width), F32)] * 2,
        core_1,
        chip_1,
        everyone,
        first,
        smem=2,
    )
    came = swap_cores(give)

    gated, sums = call(
        functools.partial(gated_kernel, heads),
        [((rows, heads * width), F32), ((n_fsdp, rows), F32)],
        core_1,
        diag,
        kept,
        came,
        maps,
        cols,
        own,
        got,
        smem=1,
    )
    sums = lax.all_to_all(sums, "fsdp", 0, 0, tiled=True)
    out = call(
        functools.partial(norm_kernel, heads * width * n_fsdp),
        [((rows, heads * width), BF16)],
        sums,
        gated,
        gain.reshape(1, -1),
    )
    return out.reshape(rows, heads, width)


def solution(mesh):
    in_specs = (
        P("ctx", "fsdp"),
        P("ctx", "fsdp", None),
        P("ctx", None),
        P("fsdp", None),
        P("fsdp"),
        P("fsdp", "ctx"),
        P("ctx"),
    )
    out_specs = P("ctx", "fsdp", None)
    return jax.shard_map(
        per_device, mesh=mesh, in_specs=in_specs, out_specs=out_specs, check_vma=False
    )
```

```python
import functools

import jax
import jax.numpy as jnp
from jax import lax
from jax.experimental import pallas as pl
from jax.experimental.pallas import tpu as pltpu
from jax.sharding import PartitionSpec as P

F32 = jnp.float32
BF16 = jnp.bfloat16
HIGH = lax.Precision.HIGHEST
PARAMS = pltpu.CompilerParams(vmem_limit_bytes=20 * 1024 * 1024)
NT = (((1,), (1,)), ((), ()))
TN = (((0,), (0,)), ((), ()))
VMEM = pl.BlockSpec(memory_space=pltpu.VMEM)
SMEM = pl.BlockSpec(memory_space=pltpu.SMEM)


def call(kernel, outs, *args, smem=0):
    shapes = [jax.ShapeDtypeStruct(s, t) for s, t in outs]
    got = pl.pallas_call(
        kernel,
        out_shape=shapes,
        in_specs=[SMEM] * smem + [VMEM] * (len(args) - smem),
        out_specs=[VMEM] * len(shapes),
        compiler_params=PARAMS,
    )(*args)
    return got[0] if len(shapes) == 1 else got


def silu(x):
    return x / (1.0 + jnp.exp(-x))


def shift(x, by):
    n = lax.axis_size("ctx")
    return lax.ppermute(x, "ctx", [(i, (i + by) % n) for i in range(n)])


def swap_cores(x):
    return lax.ppermute(x, "ctx", [(i, i ^ 1) for i in range(lax.axis_size("ctx"))])


def decay_kernel(decays_ref, starts_ref, cols_ref, decay_ref, ends_ref):
    heads, rows = decays_ref.shape
    i = lax.broadcasted_iota(jnp.int32, (rows, rows), 0)
    j = lax.broadcasted_iota(jnp.int32, (rows, rows), 1)
    causal = i >= j
    ones = causal.astype(F32)
    logs = jnp.log(decays_ref[...])
    starts = starts_ref[...].astype(F32)
    both = jnp.concatenate([logs, starts, jnp.zeros((8 - heads - 1, rows), F32)], axis=0)
    cum_row = lax.dot_general(both, ones, NT, precision=HIGH, preferred_element_type=F32)
    cum_col = lax.dot_general(ones, both, NT, precision=HIGH, preferred_element_type=F32)
    seg_row, seg_col = cum_row[heads : heads + 1], cum_col[:, heads : heads + 1]
    same = causal & (jnp.abs(seg_row - seg_col) < 0.5)
    last = cum_row[:, rows - 1 :]
    seg_last = last[heads : heads + 1]
    to_end, carry = [], []
    for h in range(heads):
        col = cum_col[:, h : h + 1]
        diff = col - cum_row[h : h + 1]
        decay_ref[h] = jnp.where(same, jnp.exp(diff), 0.0)
        total = last[h : h + 1]
        to_end.append(jnp.where(jnp.abs(seg_col - seg_last) < 0.5, jnp.exp(total - col), 0.0))
        carry.append(jnp.where(seg_col < 0.5, jnp.exp(col), 0.0))
        keep = jnp.where(seg_last < 0.5, jnp.exp(total), 0.0)
        ends_ref[h] = jnp.broadcast_to(keep, ends_ref.shape[1:])
    cols_ref[...] = jnp.concatenate(to_end + carry, axis=1)


def partial_kernel(steps, with_acc, chip_ref, tok_ref, *refs):
    blocks, outs = refs[: len(steps)], refs[len(steps) + with_acc :]
    n_chip, rows = tok_ref.shape[0], tok_ref.shape[1]
    chip = chip_ref[0]
    acc = refs[len(steps)][...] if with_acc else jnp.zeros((rows, blocks[0].shape[1]), F32)
    order = list(zip(steps, blocks))
    for at in range(0, len(order), 2):
        part = order[at : at + 2]
        toks = [tok_ref[lax.rem(chip - s + 2 * n_chip, n_chip)] for s, _ in part]
        ws = [w[...] for _, w in part]
        tok = jnp.concatenate(toks, axis=1) if len(part) > 1 else toks[0]
        w = jnp.concatenate(ws, axis=0) if len(part) > 1 else ws[0]
        acc += jnp.dot(tok, w, preferred_element_type=F32)
    if len(outs) == 1:
        outs[0][...] = acc
    else:
        outs[0][...] = acc[: rows // 2]
        outs[1][...] = acc[rows // 2 :]


def partial_product(n_out, steps, chip, tok, blocks, acc):
    shape = (tok.shape[1] // n_out, blocks[0].shape[1])
    got = call(
        functools.partial(partial_kernel, steps, len(acc)),
        [(shape, F32)] * n_out,
        chip,
        tok,
        *blocks,
        *acc,
        smem=1,
    )
    return [got] if n_out == 1 else got


def local_kernel(core_ref, own_ref, got_ref, cols_ref, ends_ref, val_ref, maps_ref, keep_ref, send_ref):
    heads, spare, width = ends_ref.shape
    n_state = keep_ref.shape[0] - spare
    n_val = heads * width
    both = own_ref[:, : n_val + 2 * n_state] + got_ref[:, : n_val + 2 * n_state]
    act = silu(both).astype(BF16)
    values = act[:, :n_val]
    maps = act[:, n_val:]
    val_ref[...] = values
    maps_ref[...] = maps
    states = []
    for h in range(heads):
        v = values[:, h * width : (h + 1) * width].astype(F32)
        scaled = (cols_ref[:, h : h + 1] * v).astype(BF16)
        states.append(
            lax.dot_general(maps[:, :n_state], scaled, TN, preferred_element_type=F32)
        )
    even = core_ref[0] == 0
    keep_ref[:n_state] = jnp.where(even, states[0], states[1])
    send_ref[:n_state] = jnp.where(even, states[1], states[0])
    keep_ref[n_state:] = jnp.where(even, ends_ref[0], ends_ref[1])
    send_ref[n_state:] = jnp.where(even, ends_ref[1], ends_ref[0])


def chip_kernel(core_ref, keep_ref, got_ref, first_ref, packed_ref):
    spare = packed_ref.shape[0] - 16
    even = core_ref[0] == 0
    keep, got = keep_ref[...], got_ref[...]
    first, second = jnp.where(even, keep, got), jnp.where(even, got, keep)
    first_ref[...] = first
    s0, g0 = first[:spare], first[spare : spare + 1]
    s1, g1 = second[:spare], second[spare : spare + 1]
    packed_ref[:spare] = (g1 * s0 + s1).astype(BF16)
    gate = jnp.broadcast_to(g0 * g1, (16, s0.shape[1]))
    hi = gate.astype(BF16).astype(F32)
    mid = (gate - hi).astype(BF16).astype(F32)
    low = gate - hi - mid
    row = lax.broadcasted_iota(jnp.int32, gate.shape, 0)
    parts = jnp.where(row == 0, hi, jnp.where(row == 1, mid, jnp.where(row == 2, low, 0.0)))
    packed_ref[spare:] = parts.astype(BF16)


def incoming_kernel(core_ref, chip_ref, all_ref, first_ref, keep_ref, give_ref):
    n_chip, n_state = all_ref.shape[0], keep_ref.shape[0]
    chip = chip_ref[0]
    state = jnp.zeros(keep_ref.shape, F32)
    for z in range(n_chip - 1):
        parts = all_ref[z, n_state:].astype(F32)
        gate = parts[0:1] + parts[1:2] + parts[2:3]
        later = gate * state + all_ref[z, :n_state].astype(F32)
        state = jnp.where(z < chip, later, state)
    second = first_ref[n_state : n_state + 1] * state + first_ref[:n_state]
    even = core_ref[0] == 0
    keep_ref[...] = jnp.where(even, state, second)
    give_ref[...] = jnp.where(even, second, state)


def diag_kernel(skip_ref, maps_ref, val_ref, decay_ref, out_ref):
    heads = decay_ref.shape[0]
    n_state = maps_ref.shape[1] // 2
    width = val_ref.shape[1] // heads
    scores = lax.dot_general(
        maps_ref[:, n_state:], maps_ref[:, :n_state], NT, preferred_element_type=F32
    )
    for h in range(heads):
        at = slice(h * width, (h + 1) * width)
        v = val_ref[:, at]
        weights = (decay_ref[h] * scores).astype(BF16)
        out = jnp.dot(weights, v, preferred_element_type=F32)
        out_ref[:, at] = out + skip_ref[h] * v.astype(F32)


def gated_kernel(heads, core_ref, diag_ref, kept_ref, came_ref, maps_ref, cols_ref, gate_ref, got_ref, out_ref, sum_ref):
    rows = diag_ref.shape[0]
    width = diag_ref.shape[1] // heads
    n_state = maps_ref.shape[1] // 2
    core = core_ref[0]
    c_map = maps_ref[:, n_state:]
    kept, came = kept_ref[...], came_ref[...]
    n_gate = gate_ref.shape[1] - heads * width
    gate = (gate_ref[:, n_gate:] + got_ref[:, n_gate:]).astype(BF16).astype(F32)
    gate = silu(gate)
    total = jnp.zeros((rows, width), F32)
    for h in range(heads):
        at = slice(h * width, (h + 1) * width)
        state = jnp.where(core == h, kept, came)
        hi = state.astype(BF16)
        lo = (state - hi.astype(F32)).astype(BF16)
        off = jnp.dot(c_map, hi, preferred_element_type=F32)
        off += jnp.dot(c_map, lo, preferred_element_type=F32)
        out = diag_ref[:, at] + off * cols_ref[:, heads + h : heads + h + 1]
        gated = out * gate[:, at]
        out_ref[:, at] = gated
        total += gated * gated
    ones = jnp.ones((sum_ref.shape[0], width), F32)
    sum_ref[...] = lax.dot_general(ones, total, NT, precision=HIGH, preferred_element_type=F32)


def norm_kernel(count, sum_ref, gated_ref, gain_ref, out_ref):
    ones = jnp.ones((sum_ref.shape[0], gated_ref.shape[1]), F32)
    mean = lax.dot_general(sum_ref[...], ones, TN, precision=HIGH, preferred_element_type=F32)
    scale = lax.rsqrt(mean / count + 1e-05)
    out_ref[...] = (gated_ref[...] * scale * gain_ref[...]).astype(BF16)


def per_device(tokens, w_xz, w_bc, gain, skip, decays, boundaries):
    rows = tokens.shape[0]
    depth, heads = w_xz.shape[:2]
    width = w_xz.shape[2] // 2
    n_state = w_bc.shape[1] // 2
    n_ctx, n_fsdp = lax.axis_size("ctx"), lax.axis_size("fsdp")
    n_chip = n_ctx // 2
    ctx = lax.axis_index("ctx")
    core, chip = ctx % 2, ctx // 2
    same_core = [[2 * z + c for z in range(n_chip)] for c in range(2)]
    core_1, chip_1 = core.reshape(1), chip.reshape(1)

    def mine_other(a, b):
        return jnp.where(core == 0, a, b), jnp.where(core == 0, b, a)

    tok_mine, tok_other = mine_other(tokens[:, :depth], tokens[:, depth:])
    tok = jnp.concatenate([tok_mine, swap_cores(tok_other)], axis=0)
    copies = jnp.broadcast_to(tok[None], (n_fsdp,) + tok.shape)
    tok = lax.all_to_all(copies, "fsdp", 0, 0)

    block = jnp.concatenate(
        [w_xz[:, :, :width].reshape(depth, -1), w_bc, w_xz[:, :, width:].reshape(depth, -1)], axis=1
    )
    n_val = heads * width
    cols, decay, ends = call(
        decay_kernel,
        [((rows, 2 * heads), F32), ((heads, rows, rows), F32), ((heads, 8, width), F32)],
        decays,
        boundaries.reshape(1, rows),
    )
    half = n_chip // 2
    up = down = block
    steps, blocks, acc = [0], [block], ()
    for s in range(1, half + 1):
        if s == half - 1:
            up, done = lax.optimization_barrier((up, acc[0]))
            acc = [done]
        up = shift(up, 2)
        steps.append(s)
        blocks.append(up)
        if s < half:
            down = shift(down, -2)
            steps.append(-s)
            blocks.append(down)
        if s == half - 4:
            acc = partial_product(1, steps, chip_1, tok, blocks, acc)
            steps, blocks = [], []
    own, other = partial_product(2, steps, chip_1, tok, blocks, acc)
    got = swap_cores(other)

    state = ((n_state + 8, width), F32)
    values, maps, keep, send = call(
        local_kernel,
        [((rows, n_val), BF16), ((rows, 2 * n_state), BF16), state, state],
        core_1,
        own,
        got,
        cols,
        ends,
        smem=1,
    )
    came = swap_cores(send)
    diag = call(diag_kernel, [((rows, n_val), F32)], skip, maps, values, decay, smem=1)
    first, packed = call(
        chip_kernel, [state, ((n_state + 16, width), BF16)], core_1, keep, came, smem=1
    )
    everyone = lax.all_gather(packed, "ctx", axis=0, axis_index_groups=same_core)
    kept, give = call(
        incoming_kernel,
        [((n_state, width), F32)] * 2,
        core_1,
        chip_1,
        everyone,
        first,
        smem=2,
    )
    came = swap_cores(give)

    gated, sums = call(
        functools.partial(gated_kernel, heads),
        [((rows, heads * width), F32), ((n_fsdp, rows), F32)],
        core_1,
        diag,
        kept,
        came,
        maps,
        cols,
        own,
        got,
        smem=1,
    )
    sums = lax.all_to_all(sums, "fsdp", 0, 0, tiled=True)
    out = call(
        functools.partial(norm_kernel, heads * width * n_fsdp),
        [((rows, heads * width), BF16)],
        sums,
        gated,
        gain.reshape(1, -1),
    )
    return out.reshape(rows, heads, width)


def solution(mesh):
    in_specs = (
        P("ctx", "fsdp"),
        P("ctx", "fsdp", None),
        P("ctx", None),
        P("fsdp", None),
        P("fsdp"),
        P("fsdp", "ctx"),
        P("ctx"),
    )
    out_specs = P("ctx", "fsdp", None)
    return jax.shard_map(
        per_device, mesh=mesh, in_specs=in_specs, out_specs=out_specs, check_vma=False
    )
```

```python
import functools

import jax
import jax.numpy as jnp
from jax import lax
from jax.experimental import pallas as pl
from jax.experimental.pallas import tpu as pltpu
from jax.sharding import PartitionSpec as P

F32 = jnp.float32
BF16 = jnp.bfloat16
HIGH = lax.Precision.HIGHEST
PARAMS = pltpu.CompilerParams(vmem_limit_bytes=20 * 1024 * 1024)
NT = (((1,), (1,)), ((), ()))
TN = (((0,), (0,)), ((), ()))
VMEM = pl.BlockSpec(memory_space=pltpu.VMEM)
SMEM = pl.BlockSpec(memory_space=pltpu.SMEM)


def call(kernel, outs, *args, smem=0):
    shapes = [jax.ShapeDtypeStruct(s, t) for s, t in outs]
    got = pl.pallas_call(
        kernel,
        out_shape=shapes,
        in_specs=[SMEM] * smem + [VMEM] * (len(args) - smem),
        out_specs=[VMEM] * len(shapes),
        compiler_params=PARAMS,
    )(*args)
    return got[0] if len(shapes) == 1 else got


def silu(x):
    return x / (1.0 + jnp.exp(-x))


def shift(x, by):
    n = lax.axis_size("ctx")
    return lax.ppermute(x, "ctx", [(i, (i + by) % n) for i in range(n)])


def swap_cores(x):
    return lax.ppermute(x, "ctx", [(i, i ^ 1) for i in range(lax.axis_size("ctx"))])


def decay_kernel(decays_ref, starts_ref, cols_ref, decay_ref, ends_ref):
    heads, rows = decays_ref.shape
    i = lax.broadcasted_iota(jnp.int32, (rows, rows), 0)
    j = lax.broadcasted_iota(jnp.int32, (rows, rows), 1)
    causal = i >= j
    ones = causal.astype(F32)
    logs = jnp.log(decays_ref[...])
    starts = starts_ref[...].astype(F32)
    both = jnp.concatenate([logs, starts, jnp.zeros((8 - heads - 1, rows), F32)], axis=0)
    cum_row = lax.dot_general(both, ones, NT, precision=HIGH, preferred_element_type=F32)
    cum_col = lax.dot_general(ones, both, NT, precision=HIGH, preferred_element_type=F32)
    seg_row, seg_col = cum_row[heads : heads + 1], cum_col[:, heads : heads + 1]
    same = causal & (jnp.abs(seg_row - seg_col) < 0.5)
    last = cum_row[:, rows - 1 :]
    seg_last = last[heads : heads + 1]
    to_end, carry = [], []
    for h in range(heads):
        col = cum_col[:, h : h + 1]
        diff = col - cum_row[h : h + 1]
        decay_ref[h] = jnp.where(same, jnp.exp(diff), 0.0)
        total = last[h : h + 1]
        to_end.append(jnp.where(jnp.abs(seg_col - seg_last) < 0.5, jnp.exp(total - col), 0.0))
        carry.append(jnp.where(seg_col < 0.5, jnp.exp(col), 0.0))
        keep = jnp.where(seg_last < 0.5, jnp.exp(total), 0.0)
        ends_ref[h] = jnp.broadcast_to(keep, ends_ref.shape[1:])
    cols_ref[...] = jnp.concatenate(to_end + carry, axis=1)


def partial_kernel(steps, with_acc, chip_ref, tok_ref, *refs):
    blocks, outs = refs[: len(steps)], refs[len(steps) + with_acc :]
    n_chip, rows = tok_ref.shape[0], tok_ref.shape[1]
    chip = chip_ref[0]
    acc = refs[len(steps)][...] if with_acc else jnp.zeros((rows, blocks[0].shape[1]), F32)
    order = list(zip(steps, blocks))
    for at in range(0, len(order), 2):
        part = order[at : at + 2]
        toks = [tok_ref[lax.rem(chip - s + 2 * n_chip, n_chip)] for s, _ in part]
        ws = [w[...] for _, w in part]
        tok = jnp.concatenate(toks, axis=1) if len(part) > 1 else toks[0]
        w = jnp.concatenate(ws, axis=0) if len(part) > 1 else ws[0]
        acc += jnp.dot(tok, w, preferred_element_type=F32)
    if len(outs) == 1:
        outs[0][...] = acc
    else:
        outs[0][...] = acc[: rows // 2]
        outs[1][...] = acc[rows // 2 :]


def partial_product(n_out, steps, chip, tok, blocks, acc):
    shape = (tok.shape[1] // n_out, blocks[0].shape[1])
    got = call(
        functools.partial(partial_kernel, steps, len(acc)),
        [(shape, F32)] * n_out,
        chip,
        tok,
        *blocks,
        *acc,
        smem=1,
    )
    return [got] if n_out == 1 else got


def three_parts(gates):
    rows = []
    for gate in gates:
        hi = gate.astype(BF16).astype(F32)
        mid = (gate - hi).astype(BF16).astype(F32)
        rows += [hi, mid, gate - hi - mid]
    index = lax.broadcasted_iota(jnp.int32, (16, gates[0].shape[1]), 0)
    out = jnp.zeros(index.shape, F32)
    for at, row in enumerate(rows):
        out = jnp.where(index == at, row, out)
    return out.astype(BF16)


def gate_of(parts, at):
    parts = parts.astype(F32)
    return parts[3 * at : 3 * at + 1] + parts[3 * at + 1 : 3 * at + 2] + parts[3 * at + 2 : 3 * at + 3]


def local_kernel(own_ref, got_ref, cols_ref, ends_ref, val_ref, maps_ref, state_ref):
    heads, _, width = ends_ref.shape
    n_state = maps_ref.shape[1] // 2
    n_val = heads * width
    both = own_ref[:, : n_val + 2 * n_state] + got_ref[:, : n_val + 2 * n_state]
    act = silu(both).astype(BF16)
    values = act[:, :n_val]
    maps = act[:, n_val:]
    val_ref[...] = values
    maps_ref[...] = maps
    for h in range(heads):
        v = values[:, h * width : (h + 1) * width].astype(F32)
        scaled = (cols_ref[:, h : h + 1] * v).astype(BF16)
        state = lax.dot_general(maps[:, :n_state], scaled, TN, preferred_element_type=F32)
        state_ref[h * n_state : (h + 1) * n_state] = state.astype(BF16)
    state_ref[heads * n_state :] = three_parts([ends_ref[h, 0:1] for h in range(heads)])


def quad_kernel(heads, place_ref, quad_ref, out_ref):
    members, rows = quad_ref.shape[0], quad_ref.shape[1] - 16
    share = rows // members
    place = place_ref[0]
    at = pl.ds(pl.multiple_of(place * share, share), share)
    state = jnp.zeros((share, quad_ref.shape[2]), F32)
    kept = jnp.ones((1, quad_ref.shape[2]), F32)
    for i in range(members):
        parts = quad_ref[i, rows:]
        gate = gate_of(parts, 0)
        for h in range(1, heads):
            gate = jnp.where(place * heads >= h * members, gate_of(parts, h), gate)
        state = gate * state + quad_ref[i, at].astype(F32)
        kept = gate * kept
    state, parts = state.astype(BF16), three_parts([kept])
    for p in range(out_ref.shape[0]):
        out_ref[p, :share] = state
        out_ref[p, share:] = parts


def before_kernel(quad_place_ref, all_ref, out_ref):
    share = out_ref.shape[0]
    mine = quad_place_ref[0]
    state = jnp.zeros(out_ref.shape, F32)
    for p in range(all_ref.shape[0] - 1):
        later = gate_of(all_ref[p, share:], 0) * state + all_ref[p, :share].astype(F32)
        state = jnp.where(p < mine, later, state)
    out_ref[...] = state


def diag_kernel(skip_ref, maps_ref, val_ref, decay_ref, out_ref):
    heads = decay_ref.shape[0]
    n_state = maps_ref.shape[1] // 2
    width = val_ref.shape[1] // heads
    scores = lax.dot_general(
        maps_ref[:, n_state:], maps_ref[:, :n_state], NT, preferred_element_type=F32
    )
    for h in range(heads):
        at = slice(h * width, (h + 1) * width)
        v = val_ref[:, at]
        weights = (decay_ref[h] * scores).astype(BF16)
        out = jnp.dot(weights, v, preferred_element_type=F32)
        out_ref[:, at] = out + skip_ref[h] * v.astype(F32)


def gated_kernel(heads, place_ref, diag_ref, quad_ref, before_ref, maps_ref, cols_ref, gate_ref, got_ref, out_ref, sum_ref):
    rows = diag_ref.shape[0]
    width = diag_ref.shape[1] // heads
    n_state = maps_ref.shape[1] // 2
    place = place_ref[0]
    c_map = maps_ref[:, n_state:]
    n_gate = gate_ref.shape[1] - heads * width
    gate = (gate_ref[:, n_gate:] + got_ref[:, n_gate:]).astype(BF16).astype(F32)
    gate = silu(gate)
    total = jnp.zeros((rows, width), F32)
    for h in range(heads):
        at = slice(h * width, (h + 1) * width)
        here = slice(h * n_state, (h + 1) * n_state)
        state = before_ref[here]
        for i in range(quad_ref.shape[0] - 1):
            gate_i = gate_of(quad_ref[i, heads * n_state :], h)
            later = gate_i * state + quad_ref[i, here].astype(F32)
            state = jnp.where(i < place, later, state)
        hi = state.astype(BF16)
        lo = (state - hi.astype(F32)).astype(BF16)
        off = jnp.dot(c_map, hi, preferred_element_type=F32)
        off += jnp.dot(c_map, lo, preferred_element_type=F32)
        out = diag_ref[:, at] + off * cols_ref[:, heads + h : heads + h + 1]
        gated = out * gate[:, at]
        out_ref[:, at] = gated
        total += gated * gated
    ones = jnp.ones((sum_ref.shape[0], width), F32)
    sum_ref[...] = lax.dot_general(ones, total, NT, precision=HIGH, preferred_element_type=F32)


def norm_kernel(count, sum_ref, gated_ref, gain_ref, out_ref):
    ones = jnp.ones((sum_ref.shape[0], gated_ref.shape[1]), F32)
    mean = lax.dot_general(sum_ref[...], ones, TN, precision=HIGH, preferred_element_type=F32)
    scale = lax.rsqrt(mean / count + 1e-05)
    out_ref[...] = (gated_ref[...] * scale * gain_ref[...]).astype(BF16)


def per_device(tokens, w_xz, w_bc, gain, skip, decays, boundaries):
    rows = tokens.shape[0]
    depth, heads = w_xz.shape[:2]
    width = w_xz.shape[2] // 2
    n_state = w_bc.shape[1] // 2
    n_ctx, n_fsdp = lax.axis_size("ctx"), lax.axis_size("fsdp")
    n_chip = n_ctx // 2
    ctx = lax.axis_index("ctx")
    core, chip = ctx % 2, ctx // 2
    chip_1 = chip.reshape(1)

    def mine_other(a, b):
        return jnp.where(core == 0, a, b), jnp.where(core == 0, b, a)

    tok_mine, tok_other = mine_other(tokens[:, :depth], tokens[:, depth:])
    tok = jnp.concatenate([tok_mine, swap_cores(tok_other)], axis=0)
    copies = jnp.broadcast_to(tok[None], (n_fsdp,) + tok.shape)
    tok = lax.all_to_all(copies, "fsdp", 0, 0)

    block = jnp.concatenate(
        [w_xz[:, :, :width].reshape(depth, -1), w_bc, w_xz[:, :, width:].reshape(depth, -1)], axis=1
    )
    n_val = heads * width
    cols, decay, ends = call(
        decay_kernel,
        [((rows, 2 * heads), F32), ((heads, rows, rows), F32), ((heads, 8, width), F32)],
        decays,
        boundaries.reshape(1, rows),
    )
    half = n_chip // 2
    up = down = block
    steps, blocks, acc = [0], [block], ()
    for s in range(1, half + 1):
        if s == half - 1:
            up, done = lax.optimization_barrier((up, acc[0]))
            acc = [done]
        up = shift(up, 2)
        steps.append(s)
        blocks.append(up)
        if s < half:
            down = shift(down, -2)
            steps.append(-s)
            blocks.append(down)
        if s == half - 4:
            acc = partial_product(1, steps, chip_1, tok, blocks, acc)
            steps, blocks = [], []
    own, other = partial_product(2, steps, chip_1, tok, blocks, acc)
    got = swap_cores(other)

    place, quad_place = (ctx % 4).reshape(1), (ctx // 4).reshape(1)
    n_quad = n_ctx // 4
    quads = [[4 * p + q for q in range(4)] for p in range(n_quad)]
    across = [[4 * p + q for p in range(n_quad)] for q in range(4)]
    values, maps, state = call(
        local_kernel,
        [
            ((rows, n_val), BF16),
            ((rows, 2 * n_state), BF16),
            ((heads * n_state + 16, width), BF16),
        ],
        own,
        got,
        cols,
        ends,
    )
    quad = lax.all_gather(state, "ctx", axis=0, axis_index_groups=quads)
    share = heads * n_state // 4
    totals = call(
        functools.partial(quad_kernel, heads),
        [((n_quad, share + 16, width), BF16)],
        place,
        quad,
        smem=1,
    )
    totals = lax.all_to_all(totals, "ctx", 0, 0, axis_index_groups=across)
    diag = call(diag_kernel, [((rows, n_val), F32)], skip, maps, values, decay, smem=1)
    before = call(before_kernel, [((share, width), F32)], quad_place, totals, smem=1)
    before = lax.all_gather(before, "ctx", axis=0, tiled=True, axis_index_groups=quads)

    gated, sums = call(
        functools.partial(gated_kernel, heads),
        [((rows, heads * width), F32), ((n_fsdp, rows), F32)],
        place,
        diag,
        quad,
        before,
        maps,
        cols,
        own,
        got,
        smem=1,
    )
    sums = lax.all_to_all(sums, "fsdp", 0, 0, tiled=True)
    out = call(
        functools.partial(norm_kernel, heads * width * n_fsdp),
        [((rows, heads * width), BF16)],
        sums,
        gated,
        gain.reshape(1, -1),
    )
    return out.reshape(rows, heads, width)


def solution(mesh):
    in_specs = (
        P("ctx", "fsdp"),
        P("ctx", "fsdp", None),
        P("ctx", None),
        P("fsdp", None),
        P("fsdp"),
        P("fsdp", "ctx"),
        P("ctx"),
    )
    out_specs = P("ctx", "fsdp", None)
    return jax.shard_map(
        per_device, mesh=mesh, in_specs=in_specs, out_specs=out_specs, check_vma=False
    )
```

```python
import functools

import jax
import jax.numpy as jnp
from jax import lax
from jax.experimental import pallas as pl
from jax.experimental.pallas import tpu as pltpu
from jax.sharding import PartitionSpec as P

F32 = jnp.float32
BF16 = jnp.bfloat16
HIGH = lax.Precision.HIGHEST
PARAMS = pltpu.CompilerParams(vmem_limit_bytes=20 * 1024 * 1024)
NT = (((1,), (1,)), ((), ()))
TN = (((0,), (0,)), ((), ()))
VMEM = pl.BlockSpec(memory_space=pltpu.VMEM)
SMEM = pl.BlockSpec(memory_space=pltpu.SMEM)


def call(kernel, outs, *args, smem=0):
    shapes = [jax.ShapeDtypeStruct(s, t) for s, t in outs]
    got = pl.pallas_call(
        kernel,
        out_shape=shapes,
        in_specs=[SMEM] * smem + [VMEM] * (len(args) - smem),
        out_specs=[VMEM] * len(shapes),
        compiler_params=PARAMS,
    )(*args)
    return got[0] if len(shapes) == 1 else got


def silu(x):
    return x / (1.0 + jnp.exp(-x))


def shift(x, by):
    n = lax.axis_size("ctx")
    return lax.ppermute(x, "ctx", [(i, (i + by) % n) for i in range(n)])


def swap_cores(x):
    return lax.ppermute(x, "ctx", [(i, i ^ 1) for i in range(lax.axis_size("ctx"))])


def decay_kernel(decays_ref, starts_ref, cols_ref, decay_ref, ends_ref):
    heads, rows = decays_ref.shape
    i = lax.broadcasted_iota(jnp.int32, (rows, rows), 0)
    j = lax.broadcasted_iota(jnp.int32, (rows, rows), 1)
    causal = i >= j
    ones = causal.astype(F32)
    logs = jnp.log(decays_ref[...])
    starts = starts_ref[...].astype(F32)
    both = jnp.concatenate([logs, starts, jnp.zeros((8 - heads - 1, rows), F32)], axis=0)
    cum_row = lax.dot_general(both, ones, NT, precision=HIGH, preferred_element_type=F32)
    cum_col = lax.dot_general(ones, both, NT, precision=HIGH, preferred_element_type=F32)
    seg_row, seg_col = cum_row[heads : heads + 1], cum_col[:, heads : heads + 1]
    same = causal & (jnp.abs(seg_row - seg_col) < 0.5)
    last = cum_row[:, rows - 1 :]
    seg_last = last[heads : heads + 1]
    to_end, carry = [], []
    for h in range(heads):
        col = cum_col[:, h : h + 1]
        diff = col - cum_row[h : h + 1]
        decay_ref[h] = jnp.where(same, jnp.exp(diff), 0.0)
        total = last[h : h + 1]
        to_end.append(jnp.where(jnp.abs(seg_col - seg_last) < 0.5, jnp.exp(total - col), 0.0))
        carry.append(jnp.where(seg_col < 0.5, jnp.exp(col), 0.0))
        keep = jnp.where(seg_last < 0.5, jnp.exp(total), 0.0)
        ends_ref[h] = jnp.broadcast_to(keep, ends_ref.shape[1:])
    cols_ref[...] = jnp.concatenate(to_end + carry, axis=1)


def partial_kernel(steps, with_acc, chip_ref, tok_ref, *refs):
    blocks, outs = refs[: len(steps)], refs[len(steps) + with_acc :]
    n_chip, rows = tok_ref.shape[0], tok_ref.shape[1]
    chip = chip_ref[0]
    acc = refs[len(steps)][...] if with_acc else jnp.zeros((rows, blocks[0].shape[1]), F32)
    order = list(zip(steps, blocks))
    for at in range(0, len(order), 2):
        part = order[at : at + 2]
        toks = [tok_ref[lax.rem(chip - s + 2 * n_chip, n_chip)] for s, _ in part]
        ws = [w[...] for _, w in part]
        tok = jnp.concatenate(toks, axis=1) if len(part) > 1 else toks[0]
        w = jnp.concatenate(ws, axis=0) if len(part) > 1 else ws[0]
        acc += jnp.dot(tok, w, preferred_element_type=F32)
    if len(outs) == 1:
        outs[0][...] = acc
    else:
        edge = outs[0].shape[1]
        outs[0][...] = acc[: rows // 2, :edge]
        outs[1][...] = acc[rows // 2 :, :edge]
        outs[2][...] = acc[: rows // 2, edge:]
        outs[3][...] = acc[rows // 2 :, edge:]


def partial_product(shapes, steps, chip, tok, blocks, acc):
    got = call(
        functools.partial(partial_kernel, steps, len(acc)),
        [(shape, F32) for shape in shapes],
        chip,
        tok,
        *blocks,
        *acc,
        smem=1,
    )
    return [got] if len(shapes) == 1 else got


def three_parts(gates):
    rows = []
    for gate in gates:
        hi = gate.astype(BF16).astype(F32)
        mid = (gate - hi).astype(BF16).astype(F32)
        rows += [hi, mid, gate - hi - mid]
    index = lax.broadcasted_iota(jnp.int32, (16, gates[0].shape[1]), 0)
    out = jnp.zeros(index.shape, F32)
    for at, row in enumerate(rows):
        out = jnp.where(index == at, row, out)
    return out.astype(BF16)


def gate_of(parts, at):
    parts = parts.astype(F32)
    return parts[3 * at : 3 * at + 1] + parts[3 * at + 1 : 3 * at + 2] + parts[3 * at + 2 : 3 * at + 3]


def local_kernel(own_ref, got_ref, cols_ref, ends_ref, val_ref, maps_ref, state_ref):
    heads, _, width = ends_ref.shape
    n_state = maps_ref.shape[1] // 2
    n_val = heads * width
    act = silu(own_ref[...] + got_ref[...]).astype(BF16)
    values = act[:, :n_val]
    maps = act[:, n_val:]
    val_ref[...] = values
    maps_ref[...] = maps
    for h in range(heads):
        v = values[:, h * width : (h + 1) * width].astype(F32)
        scaled = (cols_ref[:, h : h + 1] * v).astype(BF16)
        state = lax.dot_general(maps[:, :n_state], scaled, TN, preferred_element_type=F32)
        state_ref[h * n_state : (h + 1) * n_state] = state.astype(BF16)
    state_ref[heads * n_state :] = three_parts([ends_ref[h, 0:1] for h in range(heads)])


def quad_kernel(heads, place_ref, quad_ref, out_ref):
    members, rows = quad_ref.shape[0], quad_ref.shape[1] - 16
    share = rows // members
    place = place_ref[0]
    at = pl.ds(pl.multiple_of(place * share, share), share)
    state = jnp.zeros((share, quad_ref.shape[2]), F32)
    kept = jnp.ones((1, quad_ref.shape[2]), F32)
    for i in range(members):
        parts = quad_ref[i, rows:]
        gate = gate_of(parts, 0)
        for h in range(1, heads):
            gate = jnp.where(place * heads >= h * members, gate_of(parts, h), gate)
        state = gate * state + quad_ref[i, at].astype(F32)
        kept = gate * kept
    state, parts = state.astype(BF16), three_parts([kept])
    for p in range(out_ref.shape[0]):
        out_ref[p, :share] = state
        out_ref[p, share:] = parts


def before_kernel(quad_place_ref, all_ref, out_ref):
    share = out_ref.shape[0]
    mine = quad_place_ref[0]
    state = jnp.zeros(out_ref.shape, F32)
    for p in range(all_ref.shape[0] - 1):
        later = gate_of(all_ref[p, share:], 0) * state + all_ref[p, :share].astype(F32)
        state = jnp.where(p < mine, later, state)
    out_ref[...] = state


def diag_kernel(skip_ref, maps_ref, val_ref, decay_ref, out_ref):
    heads = decay_ref.shape[0]
    n_state = maps_ref.shape[1] // 2
    width = val_ref.shape[1] // heads
    scores = lax.dot_general(
        maps_ref[:, n_state:], maps_ref[:, :n_state], NT, preferred_element_type=F32
    )
    for h in range(heads):
        at = slice(h * width, (h + 1) * width)
        v = val_ref[:, at]
        weights = (decay_ref[h] * scores).astype(BF16)
        out = jnp.dot(weights, v, preferred_element_type=F32)
        out_ref[:, at] = out + skip_ref[h] * v.astype(F32)


def gated_kernel(heads, place_ref, diag_ref, quad_ref, before_ref, maps_ref, cols_ref, gate_ref, got_ref, out_ref, sum_ref):
    rows = diag_ref.shape[0]
    width = diag_ref.shape[1] // heads
    n_state = maps_ref.shape[1] // 2
    place = place_ref[0]
    c_map = maps_ref[:, n_state:]
    gate = (gate_ref[...] + got_ref[...]).astype(BF16).astype(F32)
    gate = silu(gate)
    total = jnp.zeros((rows, width), F32)
    for h in range(heads):
        at = slice(h * width, (h + 1) * width)
        here = slice(h * n_state, (h + 1) * n_state)
        state = before_ref[here]
        for i in range(quad_ref.shape[0] - 1):
            gate_i = gate_of(quad_ref[i, heads * n_state :], h)
            later = gate_i * state + quad_ref[i, here].astype(F32)
            state = jnp.where(i < place, later, state)
        hi = state.astype(BF16)
        lo = (state - hi.astype(F32)).astype(BF16)
        off = jnp.dot(c_map, hi, preferred_element_type=F32)
        off += jnp.dot(c_map, lo, preferred_element_type=F32)
        out = diag_ref[:, at] + off * cols_ref[:, heads + h : heads + h + 1]
        gated = out * gate[:, at]
        out_ref[:, at] = gated
        total += gated * gated
    ones = jnp.ones((sum_ref.shape[0], width), F32)
    sum_ref[...] = lax.dot_general(ones, total, NT, precision=HIGH, preferred_element_type=F32)


def norm_kernel(count, sum_ref, gated_ref, gain_ref, out_ref):
    ones = jnp.ones((sum_ref.shape[0], gated_ref.shape[1]), F32)
    mean = lax.dot_general(sum_ref[...], ones, TN, precision=HIGH, preferred_element_type=F32)
    scale = lax.rsqrt(mean / count + 1e-05)
    out_ref[...] = (gated_ref[...] * scale * gain_ref[...]).astype(BF16)


def per_device(tokens, w_xz, w_bc, gain, skip, decays, boundaries):
    rows = tokens.shape[0]
    depth, heads = w_xz.shape[:2]
    width = w_xz.shape[2] // 2
    n_state = w_bc.shape[1] // 2
    n_ctx, n_fsdp = lax.axis_size("ctx"), lax.axis_size("fsdp")
    n_chip = n_ctx // 2
    ctx = lax.axis_index("ctx")
    core, chip = ctx % 2, ctx // 2
    chip_1 = chip.reshape(1)

    def mine_other(a, b):
        return jnp.where(core == 0, a, b), jnp.where(core == 0, b, a)

    tok_mine, tok_other = mine_other(tokens[:, :depth], tokens[:, depth:])
    tok = jnp.concatenate([tok_mine, swap_cores(tok_other)], axis=0)
    copies = jnp.broadcast_to(tok[None], (n_fsdp,) + tok.shape)
    tok = lax.all_to_all(copies, "fsdp", 0, 0)

    block = jnp.concatenate(
        [w_xz[:, :, :width].reshape(depth, -1), w_bc, w_xz[:, :, width:].reshape(depth, -1)], axis=1
    )
    n_val = heads * width
    cols, decay, ends = call(
        decay_kernel,
        [((rows, 2 * heads), F32), ((heads, rows, rows), F32), ((heads, 8, width), F32)],
        decays,
        boundaries.reshape(1, rows),
    )
    half = n_chip // 2
    up = down = block
    steps, blocks, acc = [0], [block], ()
    for s in range(1, half + 1):
        if s == half - 1:
            up, done = lax.optimization_barrier((up, acc[0]))
            acc = [done]
        up = shift(up, 2)
        steps.append(s)
        blocks.append(up)
        if s < half:
            down = shift(down, -2)
            steps.append(-s)
            blocks.append(down)
        if s == half - 4:
            acc = partial_product([(2 * rows, block.shape[1])], steps, chip_1, tok, blocks, acc)
            steps, blocks = [], []
    n_first = n_val + 2 * n_state
    shapes = [(rows, n_first)] * 2 + [(rows, n_val)] * 2
    own, other, gate_own, gate_other = partial_product(shapes, steps, chip_1, tok, blocks, acc)
    got = swap_cores(other)

    place, quad_place = (ctx % 4).reshape(1), (ctx // 4).reshape(1)
    n_quad = n_ctx // 4
    quads = [[4 * p + q for q in range(4)] for p in range(n_quad)]
    across = [[4 * p + q for p in range(n_quad)] for q in range(4)]
    values, maps, state = call(
        local_kernel,
        [
            ((rows, n_val), BF16),
            ((rows, 2 * n_state), BF16),
            ((heads * n_state + 16, width), BF16),
        ],
        own,
        got,
        cols,
        ends,
    )
    quad = lax.all_gather(state, "ctx", axis=0, axis_index_groups=quads)
    share = heads * n_state // 4
    totals = call(
        functools.partial(quad_kernel, heads),
        [((n_quad, share + 16, width), BF16)],
        place,
        quad,
        smem=1,
    )
    totals = lax.all_to_all(totals, "ctx", 0, 0, axis_index_groups=across)
    diag = call(diag_kernel, [((rows, n_val), F32)], skip, maps, values, decay, smem=1)
    gate_other, diag = lax.optimization_barrier((gate_other, diag))
    gate_got = swap_cores(gate_other)
    before = call(before_kernel, [((share, width), F32)], quad_place, totals, smem=1)
    before = lax.all_gather(before, "ctx", axis=0, tiled=True, axis_index_groups=quads)

    gated, sums = call(
        functools.partial(gated_kernel, heads),
        [((rows, heads * width), F32), ((n_fsdp, rows), F32)],
        place,
        diag,
        quad,
        before,
        maps,
        cols,
        gate_own,
        gate_got,
        smem=1,
    )
    sums = lax.all_to_all(sums, "fsdp", 0, 0, tiled=True)
    out = call(
        functools.partial(norm_kernel, heads * width * n_fsdp),
        [((rows, heads * width), BF16)],
        sums,
        gated,
        gain.reshape(1, -1),
    )
    return out.reshape(rows, heads, width)


def solution(mesh):
    in_specs = (
        P("ctx", "fsdp"),
        P("ctx", "fsdp", None),
        P("ctx", None),
        P("fsdp", None),
        P("fsdp"),
        P("fsdp", "ctx"),
        P("ctx"),
    )
    out_specs = P("ctx", "fsdp", None)
    return jax.shard_map(
        per_device, mesh=mesh, in_specs=in_specs, out_specs=out_specs, check_vma=False
    )
```

```python
import functools

import jax
import jax.numpy as jnp
from jax import lax
from jax.experimental import pallas as pl
from jax.experimental.pallas import tpu as pltpu
from jax.sharding import PartitionSpec as P

F32 = jnp.float32
BF16 = jnp.bfloat16
HIGH = lax.Precision.HIGHEST
PARAMS = pltpu.CompilerParams(vmem_limit_bytes=20 * 1024 * 1024)
NT = (((1,), (1,)), ((), ()))
TN = (((0,), (0,)), ((), ()))
VMEM = pl.BlockSpec(memory_space=pltpu.VMEM)
SMEM = pl.BlockSpec(memory_space=pltpu.SMEM)


def call(kernel, outs, *args, smem=0):
    shapes = [jax.ShapeDtypeStruct(s, t) for s, t in outs]
    got = pl.pallas_call(
        kernel,
        out_shape=shapes,
        in_specs=[SMEM] * smem + [VMEM] * (len(args) - smem),
        out_specs=[VMEM] * len(shapes),
        compiler_params=PARAMS,
    )(*args)
    return got[0] if len(shapes) == 1 else got


def silu(x):
    return x / (1.0 + jnp.exp(-x))


def shift(x, by):
    n = lax.axis_size("ctx")
    return lax.ppermute(x, "ctx", [(i, (i + by) % n) for i in range(n)])


def swap_cores(x):
    return lax.ppermute(x, "ctx", [(i, i ^ 1) for i in range(lax.axis_size("ctx"))])


def decay_kernel(decays_ref, starts_ref, cols_ref, decay_ref, ends_ref):
    heads, rows = decays_ref.shape
    i = lax.broadcasted_iota(jnp.int32, (rows, rows), 0)
    j = lax.broadcasted_iota(jnp.int32, (rows, rows), 1)
    causal = i >= j
    ones = causal.astype(F32)
    logs = jnp.log(decays_ref[...])
    starts = starts_ref[...].astype(F32)
    both = jnp.concatenate([logs, starts, jnp.zeros((8 - heads - 1, rows), F32)], axis=0)
    cum_row = lax.dot_general(both, ones, NT, precision=HIGH, preferred_element_type=F32)
    cum_col = lax.dot_general(ones, both, NT, precision=HIGH, preferred_element_type=F32)
    seg_row, seg_col = cum_row[heads : heads + 1], cum_col[:, heads : heads + 1]
    same = causal & (jnp.abs(seg_row - seg_col) < 0.5)
    last = cum_row[:, rows - 1 :]
    seg_last = last[heads : heads + 1]
    to_end, carry = [], []
    for h in range(heads):
        col = cum_col[:, h : h + 1]
        diff = col - cum_row[h : h + 1]
        decay_ref[h] = jnp.where(same, jnp.exp(diff), 0.0)
        total = last[h : h + 1]
        to_end.append(jnp.where(jnp.abs(seg_col - seg_last) < 0.5, jnp.exp(total - col), 0.0))
        carry.append(jnp.where(seg_col < 0.5, jnp.exp(col), 0.0))
        keep = jnp.where(seg_last < 0.5, jnp.exp(total), 0.0)
        ends_ref[h] = jnp.broadcast_to(keep, ends_ref.shape[1:])
    cols_ref[...] = jnp.concatenate(to_end + carry, axis=1)


def partial_kernel(steps, with_acc, chip_ref, tok_ref, *refs):
    blocks, outs = refs[: len(steps)], refs[len(steps) + with_acc :]
    n_chip, rows = tok_ref.shape[0], tok_ref.shape[1]
    chip = chip_ref[0]
    acc = refs[len(steps)][...] if with_acc else jnp.zeros((rows, blocks[0].shape[1]), F32)
    order = list(zip(steps, blocks))
    for at in range(0, len(order), 2):
        part = order[at : at + 2]
        toks = [tok_ref[lax.rem(chip - s + 2 * n_chip, n_chip)] for s, _ in part]
        ws = [w[...] for _, w in part]
        tok = jnp.concatenate(toks, axis=1) if len(part) > 1 else toks[0]
        w = jnp.concatenate(ws, axis=0) if len(part) > 1 else ws[0]
        acc += jnp.dot(tok, w, preferred_element_type=F32)
    if len(outs) == 1:
        outs[0][...] = acc
    else:
        outs[0][...] = acc[: rows // 2]
        outs[1][...] = acc[rows // 2 :]


def partial_product(n_out, steps, chip, tok, blocks, acc):
    shape = (tok.shape[1] // n_out, blocks[0].shape[1])
    got = call(
        functools.partial(partial_kernel, steps, len(acc)),
        [(shape, F32)] * n_out,
        chip,
        tok,
        *blocks,
        *acc,
        smem=1,
    )
    return [got] if n_out == 1 else got


def local_kernel(core_ref, own_ref, got_ref, cols_ref, ends_ref, val_ref, maps_ref, keep_ref, send_ref):
    heads, spare, width = ends_ref.shape
    n_state = keep_ref.shape[0] - spare
    n_val = heads * width
    both = own_ref[:, : n_val + 2 * n_state] + got_ref[:, : n_val + 2 * n_state]
    act = silu(both).astype(BF16)
    values = act[:, :n_val]
    maps = act[:, n_val:]
    val_ref[...] = values
    maps_ref[...] = maps
    states = []
    for h in range(heads):
        v = values[:, h * width : (h + 1) * width].astype(F32)
        scaled = (cols_ref[:, h : h + 1] * v).astype(BF16)
        states.append(
            lax.dot_general(maps[:, :n_state], scaled, TN, preferred_element_type=F32)
        )
    even = core_ref[0] == 0
    keep_ref[:n_state] = jnp.where(even, states[0], states[1])
    send_ref[:n_state] = jnp.where(even, states[1], states[0])
    keep_ref[n_state:] = jnp.where(even, ends_ref[0], ends_ref[1])
    send_ref[n_state:] = jnp.where(even, ends_ref[1], ends_ref[0])


def chip_kernel(core_ref, keep_ref, got_ref, first_ref, packed_ref):
    spare = packed_ref.shape[0] - 16
    even = core_ref[0] == 0
    keep, got = keep_ref[...], got_ref[...]
    first, second = jnp.where(even, keep, got), jnp.where(even, got, keep)
    first_ref[...] = first
    s0, g0 = first[:spare], first[spare : spare + 1]
    s1, g1 = second[:spare], second[spare : spare + 1]
    packed_ref[:spare] = (g1 * s0 + s1).astype(BF16)
    gate = jnp.broadcast_to(g0 * g1, (16, s0.shape[1]))
    hi = gate.astype(BF16).astype(F32)
    mid = (gate - hi).astype(BF16).astype(F32)
    low = gate - hi - mid
    row = lax.broadcasted_iota(jnp.int32, gate.shape, 0)
    parts = jnp.where(row == 0, hi, jnp.where(row == 1, mid, jnp.where(row == 2, low, 0.0)))
    packed_ref[spare:] = parts.astype(BF16)


def incoming_kernel(core_ref, chip_ref, all_ref, first_ref, keep_ref, give_ref):
    n_chip, n_state = all_ref.shape[0], keep_ref.shape[0]
    chip = chip_ref[0]
    state = jnp.zeros(keep_ref.shape, F32)
    for z in range(n_chip - 1):
        parts = all_ref[z, n_state:].astype(F32)
        gate = parts[0:1] + parts[1:2] + parts[2:3]
        later = gate * state + all_ref[z, :n_state].astype(F32)
        state = jnp.where(z < chip, later, state)
    second = first_ref[n_state : n_state + 1] * state + first_ref[:n_state]
    even = core_ref[0] == 0
    keep_ref[...] = jnp.where(even, state, second)
    give_ref[...] = jnp.where(even, second, state)


def diag_kernel(skip_ref, maps_ref, val_ref, decay_ref, out_ref):
    heads = decay_ref.shape[0]
    n_state = maps_ref.shape[1] // 2
    width = val_ref.shape[1] // heads
    scores = lax.dot_general(
        maps_ref[:, n_state:], maps_ref[:, :n_state], NT, preferred_element_type=F32
    )
    for h in range(heads):
        at = slice(h * width, (h + 1) * width)
        v = val_ref[:, at]
        weights = (decay_ref[h] * scores).astype(BF16)
        out = jnp.dot(weights, v, preferred_element_type=F32)
        out_ref[:, at] = out + skip_ref[h] * v.astype(F32)


def gated_kernel(heads, core_ref, diag_ref, kept_ref, came_ref, maps_ref, cols_ref, gate_ref, got_ref, out_ref, sum_ref):
    rows = diag_ref.shape[0]
    width = diag_ref.shape[1] // heads
    n_state = maps_ref.shape[1] // 2
    core = core_ref[0]
    c_map = maps_ref[:, n_state:]
    kept, came = kept_ref[...], came_ref[...]
    n_gate = gate_ref.shape[1] - heads * width
    gate = (gate_ref[:, n_gate:] + got_ref[:, n_gate:]).astype(BF16).astype(F32)
    gate = silu(gate)
    total = jnp.zeros((rows, width), F32)
    for h in range(heads):
        at = slice(h * width, (h + 1) * width)
        state = jnp.where(core == h, kept, came)
        hi = state.astype(BF16)
        lo = (state - hi.astype(F32)).astype(BF16)
        off = jnp.dot(c_map, hi, preferred_element_type=F32)
        off += jnp.dot(c_map, lo, preferred_element_type=F32)
        out = diag_ref[:, at] + off * cols_ref[:, heads + h : heads + h + 1]
        gated = out * gate[:, at]
        out_ref[:, at] = gated
        total += gated * gated
    ones = jnp.ones((sum_ref.shape[0], width), F32)
    sum_ref[...] = lax.dot_general(ones, total, NT, precision=HIGH, preferred_element_type=F32)


def norm_kernel(count, sum_ref, gated_ref, gain_ref, out_ref):
    ones = jnp.ones((sum_ref.shape[0], gated_ref.shape[1]), F32)
    mean = lax.dot_general(sum_ref[...], ones, TN, precision=HIGH, preferred_element_type=F32)
    scale = lax.rsqrt(mean / count + 1e-05)
    out_ref[...] = (gated_ref[...] * scale * gain_ref[...]).astype(BF16)


def per_device(tokens, w_xz, w_bc, gain, skip, decays, boundaries):
    rows = tokens.shape[0]
    depth, heads = w_xz.shape[:2]
    width = w_xz.shape[2] // 2
    n_state = w_bc.shape[1] // 2
    n_ctx, n_fsdp = lax.axis_size("ctx"), lax.axis_size("fsdp")
    n_chip = n_ctx // 2
    ctx = lax.axis_index("ctx")
    core, chip = ctx % 2, ctx // 2
    same_core = [[2 * z + c for z in range(n_chip)] for c in range(2)]
    core_1, chip_1 = core.reshape(1), chip.reshape(1)

    tok = jnp.concatenate([tokens, swap_cores(tokens)], axis=0)
    tok = jnp.where(core == 0, tok[:, :depth], tok[:, depth:])
    copies = jnp.broadcast_to(tok[None], (n_fsdp,) + tok.shape)
    tok = lax.all_to_all(copies, "fsdp", 0, 0)

    block = jnp.concatenate(
        [w_xz[:, :, :width].reshape(depth, -1), w_bc, w_xz[:, :, width:].reshape(depth, -1)], axis=1
    )
    n_val = heads * width
    cols, decay, ends = call(
        decay_kernel,
        [((rows, 2 * heads), F32), ((heads, rows, rows), F32), ((heads, 8, width), F32)],
        decays,
        boundaries.reshape(1, rows),
    )
    half = n_chip // 2
    up = down = block
    steps, blocks, acc = [0], [block], ()
    for s in range(1, half + 1):
        up = shift(up, 2)
        steps.append(s)
        blocks.append(up)
        if s == half - 2:
            acc = partial_product(1, steps, chip_1, tok, blocks, acc)
            steps, blocks = [], []
        if s < half:
            down = shift(down, -2)
            steps.append(-s)
            blocks.append(down)
    own, other = partial_product(2, steps, chip_1, tok, blocks, acc)
    got = swap_cores(other)

    state = ((n_state + 8, width), F32)
    values, maps, keep, send = call(
        local_kernel,
        [((rows, n_val), BF16), ((rows, 2 * n_state), BF16), state, state],
        core_1,
        own,
        got,
        cols,
        ends,
        smem=1,
    )
    came = swap_cores(send)
    diag = call(diag_kernel, [((rows, n_val), F32)], skip, maps, values, decay, smem=1)
    first, packed = call(
        chip_kernel, [state, ((n_state + 16, width), BF16)], core_1, keep, came, smem=1
    )
    everyone = lax.all_gather(packed, "ctx", axis=0, axis_index_groups=same_core)
    kept, give = call(
        incoming_kernel,
        [((n_state, width), F32)] * 2,
        core_1,
        chip_1,
        everyone,
        first,
        smem=2,
    )
    came = swap_cores(give)

    gated, sums = call(
        functools.partial(gated_kernel, heads),
        [((rows, heads * width), F32), ((n_fsdp, rows), F32)],
        core_1,
        diag,
        kept,
        came,
        maps,
        cols,
        own,
        got,
        smem=1,
    )
    sums = lax.all_to_all(sums, "fsdp", 0, 0, tiled=True)
    out = call(
        functools.partial(norm_kernel, heads * width * n_fsdp),
        [((rows, heads * width), BF16)],
        sums,
        gated,
        gain.reshape(1, -1),
    )
    return out.reshape(rows, heads, width)


def solution(mesh):
    in_specs = (
        P("ctx", "fsdp"),
        P("ctx", "fsdp", None),
        P("ctx", None),
        P("fsdp", None),
        P("fsdp"),
        P("fsdp", "ctx"),
        P("ctx"),
    )
    out_specs = P("ctx", "fsdp", None)
    return jax.shard_map(
        per_device, mesh=mesh, in_specs=in_specs, out_specs=out_specs, check_vma=False
    )
```
